32 devices in a mesh: dp: 4 (over y, x), fsdp: 8 (over z, core).
Axes of the slice: x: 2, y: 2, z: 4, core: 2. Of those that a mesh axis runs over, the one named last changes fastest.
Arguments:
- inputs: bfloat16 [256, 256, 512], P(('dp', 'fsdp')), may hold values from -6 to 6
- lengths: int32 [256], P(('dp', 'fsdp')), may hold values from 64 to 250, as said below
- validity: int32 [256], P(('dp', 'fsdp')), may hold values 0 or 1
- absorbed: int32 [256, 256], P(('dp', 'fsdp')), may hold values 0 or 1
- timesteps: int32 [256], P(('dp', 'fsdp')), may hold values from 0 to 255
- attn_gain: bfloat16 [512], P(('dp', 'fsdp')), may hold values from 0.099609375 to 1.8984375
- attn_shift: bfloat16 [512], P(('dp', 'fsdp')), may hold values from -3 to 3
- query_key_value_weight: bfloat16 [512, 1536], P(('dp', 'fsdp')), may hold values from -0.25 to 0.25
- query_bias: bfloat16 [512], P(('dp', 'fsdp')), may hold values from -3 to 3
- value_bias: bfloat16 [512], P(('dp', 'fsdp')), may hold values from -3 to 3
- output_projection_weight: bfloat16 [512, 512], P(('dp', 'fsdp')), may hold values from -2 to 2
- output_projection_bias: bfloat16 [512], P(('dp', 'fsdp')), may hold values from -3 to 3
- mlp_gain: bfloat16 [512], P(('dp', 'fsdp')), may hold values from 0.099609375 to 1.8984375
- mlp_shift: bfloat16 [512], P(('dp', 'fsdp')), may hold values from -3 to 3
- up_projection_weight: bfloat16 [512, 2048], P(('dp', 'fsdp')), may hold values from -0.25 to 0.25
- hidden_units_bias: bfloat16 [2048], P(('dp', 'fsdp')), may hold values from -3 to 3
- down_projection_weight: bfloat16 [2048, 512], P(('dp', 'fsdp')), may hold values from -0.25 to 0.25
- down_output_bias: bfloat16 [512], P(('dp', 'fsdp')), may hold values from -3 to 3
- absorb_vector: bfloat16 [512], P(('dp', 'fsdp')), may hold values from -4 to 4
- time_table: bfloat16 [256, 512], P(('dp', 'fsdp')), may hold values from -4 to 4
- cotangent: bfloat16 [256, 256, 512], P(('dp', 'fsdp')), may hold values from -6 to 6
Outputs:
- output: bfloat16 [256, 256, 512], P(('dp', 'fsdp'))
- input_grad: bfloat16 [256, 256, 512], P(('dp', 'fsdp'))
- grad_attn_gain: float32 [512], P(('dp', 'fsdp'))
- grad_attn_shift: float32 [512], P(('dp', 'fsdp'))
- grad_qkv_weight: float32 [512, 1536], P(('dp', 'fsdp'))
- grad_query_bias: float32 [512], P(('dp', 'fsdp'))
- grad_value_bias: float32 [512], P(('dp', 'fsdp'))
- grad_proj_weight: float32 [512, 512], P(('dp', 'fsdp'))
- grad_proj_bias: float32 [512], P(('dp', 'fsdp'))
- grad_mlp_gain: float32 [512], P(('dp', 'fsdp'))
- grad_mlp_shift: float32 [512], P(('dp', 'fsdp'))
- grad_up_weight: float32 [512, 2048], P(('dp', 'fsdp'))
- grad_up_bias: float32 [2048], P(('dp', 'fsdp'))
- grad_down_weight: float32 [2048, 512], P(('dp', 'fsdp'))
- grad_down_bias: float32 [512], P(('dp', 'fsdp'))
- grad_absorb_vector: float32 [512], P(('dp', 'fsdp'))
- grad_time_table: float32 [256, 512], P(('dp', 'fsdp'))
The draws below stay inside these ranges and needn't reach their ends.
Inputs may be any that keep to these rules, and one draw needn't show every extreme that they name: `lengths`: each length is one of 64, 128 and 250.
All inputs are finite; a program needn't handle non-finite values. No bound on the sum of `validity` or of `absorbed` on one device may be relied on, other than what follows from the above.
Results may differ from the reference program's by a relative error of at most 0.015.
Values may be sent and summed in bfloat16 or wider, within the bound.
No kernel may reach another device: no remote copies, remote signals or barrier semaphores. Data moves between devices by JAX's collectives and lax.ppermute only.
A program may use at most 192 MiB of HBM per device.

```python
import math
import jax
import jax.numpy as jnp
from jax import lax

D = 512
HEADS = 8
HEAD_DIM = 64
FF = 2048
SLOT_LEN = 256
TSTEPS = 256
SLOTS = 256


def draw_lengths(key, part):
    key = jax.random.fold_in(key, 5)
    picked = jax.random.randint(key, (SLOTS,), 0, 3)
    choices_tab = jnp.array([SLOT_LEN // 4, SLOT_LEN // 2, SLOT_LEN - 6], dtype=jnp.int32)
    result = choices_tab[picked]
    result = result.at[0].set(SLOT_LEN - 6)
    result = result.at[1].set(SLOT_LEN // 4)
    return result.astype(jnp.int32)


def set_ends(values, rng, smallest, top_value):
    shape = values.shape
    spot = [jax.random.randint(jax.random.fold_in(rng, axis), (), 0, shape[axis]) for axis in range(len(shape))]
    values = values.at[tuple(spot)].set(smallest)
    longest = shape.index(max(shape))
    spot[longest] = (spot[longest] + 1) % shape[longest]
    return values.at[tuple(spot)].set(top_value)


def block_scale(stream_key, dims, cuts, least, largest):
    gain, own = 1.0, jax.random.fold_in(stream_key, 6)
    for axis_at, blocks in cuts:
        draws = jnp.exp(jax.random.uniform(jax.random.fold_in(own, axis_at), (blocks,), jnp.float32, least / len(cuts), largest / len(cuts)))
        gain = gain * jnp.repeat(draws, dims[axis_at] // blocks).reshape([-1 if axis == axis_at else 1 for axis in range(len(dims))])
    return gain


def bell_draw(key, dims, width, most, pieces=(), held_as=jnp.bfloat16):
    values = jax.random.normal(key, dims, jnp.float32) * width
    if len(pieces) > 0:
        values = block_scale(key, dims, pieces, -0.22, 0.18) * values
    return jnp.clip(values, min=-most, max=most).astype(held_as)


def setup_inputs(seed: int = 0) -> dict:
    key_list = jax.random.split(jax.random.key(seed), 22)
    return {
        "inputs": bell_draw(key_list[0], (SLOTS, SLOT_LEN, D), 1.0, 6.0, ((0, 32),)),
        "lengths": draw_lengths(jax.random.fold_in(key_list[21], 71), 0),
        "validity": set_ends((jax.random.randint(key_list[2], (SLOTS,), 0, 4) < 3).astype(jnp.int32), jax.random.fold_in(key_list[2], 1), 0, 1),
        "absorbed": set_ends((jax.random.randint(key_list[3], (SLOTS, SLOT_LEN), 0, 2) < 1).astype(jnp.int32), jax.random.fold_in(key_list[3], 1), 0, 1),
        "timesteps": set_ends(jax.random.randint(key_list[4], (SLOTS,), 0, TSTEPS), jax.random.fold_in(key_list[4], 1), 0, TSTEPS - 1).astype(jnp.int32),
        "attn_gain": jnp.clip(1.0 + 0.18 * jax.random.normal(key_list[5], (D,), jnp.float32), 0.099609375, 1.8984375).astype(jnp.bfloat16),
        "attn_shift": bell_draw(key_list[6], (D,), 0.5, 3.0, ((0, 32),)),
        "query_key_value_weight": bell_draw(key_list[7], (D, 3 * D), D ** -0.5, 0.25, ((0, 32),)),
        "query_bias": bell_draw(key_list[8], (D,), 0.5, 3.0, ((0, 32),)),
        "value_bias": bell_draw(key_list[9], (D,), 0.5, 3.0, ((0, 32),)),
        "output_projection_weight": bell_draw(key_list[10], (D, D), (D // 64) ** -0.5, 2.0, ((0, 32),)),
        "output_projection_bias": bell_draw(key_list[11], (D,), 0.5, 3.0, ((0, 32),)),
        "mlp_gain": jnp.clip(1.0 + 0.18 * jax.random.normal(key_list[12], (D,), jnp.float32), 0.099609375, 1.8984375).astype(jnp.bfloat16),
        "mlp_shift": bell_draw(key_list[13], (D,), 0.5, 3.0, ((0, 32),)),
        "up_projection_weight": bell_draw(key_list[14], (D, FF), D ** -0.5, 0.25, ((0, 32),)),
        "hidden_units_bias": bell_draw(key_list[15], (FF,), 0.5, 3.0, ((0, 32),)),
        "down_projection_weight": bell_draw(key_list[16], (FF, D), (FF // 4) ** -0.5, 0.25, ((0, 32),)),
        "down_output_bias": bell_draw(key_list[17], (D,), 0.5, 3.0, ((0, 32),)),
        "absorb_vector": bell_draw(key_list[18], (D,), 1.0, 4.0, ((0, 32),)),
        "time_table": bell_draw(key_list[19], (TSTEPS, D), 0.7, 4.0, ((0, 32),)),
        "cotangent": bell_draw(key_list[20], (SLOTS, SLOT_LEN, D), 1.0, 6.0, ((0, 32),)),
    }


EPS = 1e-05
NEG = -1e+30

@jax.custom_vjp
def low(v):
    return lax.optimization_barrier(v.astype(jnp.bfloat16)).astype(jnp.float32)

@jax.custom_vjp
def reduced_backward(v):
    return v

def low_keep(v):
    return (low(v), None)

def low_pass(kept, grad):
    return (grad,)

def back_keep(v):
    return (v, None)

def back_low(kept, grad):
    return (low(grad),)
low.defvjp(low_keep, low_pass)
reduced_backward.defvjp(back_keep, back_low)

def layer_norm(vector, scale_vec, shift_vec):
    centre = vector - lax.optimization_barrier(jnp.mean(vector, axis=-1, keepdims=True))
    spread = lax.optimization_barrier(jnp.mean(centre * centre, axis=-1, keepdims=True))
    return centre * lax.rsqrt(spread + EPS) * scale_vec + shift_vec

def forward_group(params, inputs_f, key_ok, row_ok, absorbed_f, steps_grp):
    attn_gain, attn_shift, query_key_value_weight, query_bias, value_bias, output_projection_weight, output_projection_bias, mlp_gain, mlp_shift, up_projection_weight, hidden_units_bias, down_projection_weight, down_output_bias, absorb_vector, time_table = params
    highest_accuracy = lax.Precision.HIGHEST
    slot_count, length, model_width = inputs_f.shape
    initial = inputs_f + absorbed_f[..., None] * absorb_vector + jnp.take(time_table, steps_grp, axis=0)[:, None, :]
    first_normalized = low(layer_norm(initial, attn_gain, attn_shift))
    stacked_query_bias = jnp.concatenate([query_bias, jnp.zeros_like(query_bias), value_bias])
    projected_attention = jnp.einsum('frp,pi->fri', first_normalized, query_key_value_weight, precision=highest_accuracy) + stacked_query_bias
    projected_attention = reduced_backward(low(projected_attention)).reshape(slot_count, length, 3, HEADS, HEAD_DIM)
    queries = projected_attention[:, :, 0]
    key_rows = projected_attention[:, :, 1]
    values = projected_attention[:, :, 2]
    scores = jnp.einsum('sqhc,skhc->shqk', queries, key_rows, precision=highest_accuracy) * HEAD_DIM ** (-0.5)
    scores = jnp.where(key_ok[:, None, None, :], reduced_backward(scores), NEG)
    soft_weights = jax.nn.softmax(scores, axis=-1)
    attention_mixture = jnp.einsum('shqk,skhc->sqhc', low(soft_weights), values, precision=highest_accuracy)
    attention_mixture = reduced_backward(low(attention_mixture.reshape(slot_count, length, model_width)))
    attention_result = reduced_backward(jnp.einsum('frp,pi->fri', attention_mixture, output_projection_weight, precision=highest_accuracy) + output_projection_bias)
    middle = initial + row_ok[..., None] * attention_result
    second_normalized2 = low(layer_norm(middle, mlp_gain, mlp_shift))
    hidden_before_gelu = reduced_backward(jnp.einsum('thm,mr->thr', second_normalized2, up_projection_weight, precision=highest_accuracy) + hidden_units_bias)
    gelu_outputs = low(jax.nn.gelu(hidden_before_gelu, approximate=True))
    layer_result = reduced_backward(jnp.einsum('jnv,vx->jnx', gelu_outputs, down_projection_weight, precision=highest_accuracy) + down_output_bias)
    return middle + row_ok[..., None] * layer_result

def reference(inputs, lengths, validity, absorbed, timesteps, attn_gain, attn_shift, query_key_value_weight, query_bias, value_bias, output_projection_weight, output_projection_bias, mlp_gain, mlp_shift, up_projection_weight, hidden_units_bias, down_projection_weight, down_output_bias, absorb_vector, time_table, cotangent):
    params = tuple((item.astype(jnp.float32) for item in (attn_gain, attn_shift, query_key_value_weight, query_bias, value_bias, output_projection_weight, output_projection_bias, mlp_gain, mlp_shift, up_projection_weight, hidden_units_bias, down_projection_weight, down_output_bias, absorb_vector, time_table)))
    position = jnp.arange(SLOT_LEN, dtype=jnp.int32)
    key_ok = position[None, :] < lengths[:, None]
    row_ok = (key_ok & (validity[:, None] > 0)).astype(jnp.float32)
    per_group = math.gcd(SLOTS, max(1, 4096 // SLOT_LEN))
    n_groups = SLOTS // per_group

    def split(array):
        return array.reshape((n_groups, per_group) + array.shape[1:])
    blocks = (split(inputs.astype(jnp.float32)), split(key_ok), split(row_ok), split(absorbed.astype(jnp.float32)), split(timesteps.astype(jnp.int32)), split(cotangent.astype(jnp.float32)))

    def step(totals, block):
        inputs_g, keys_g, rows_g, absorbed_g, steps_g, cot_g = block

        def apply(params_in, inputs_in):
            return forward_group(params_in, inputs_in, keys_g, rows_g, absorbed_g, steps_g)
        result, pullback = jax.vjp(apply, params, inputs_g)
        grad_params, grad_inputs = pullback(cot_g)
        totals = jax.tree.map(lambda left, right: left + right, totals, grad_params)
        return (totals, (result.astype(jnp.bfloat16), grad_inputs.astype(jnp.bfloat16)))
    zeros = jax.tree.map(jnp.zeros_like, params)
    totals, (results, grads) = lax.scan(step, zeros, blocks)
    output = results.reshape(SLOTS, SLOT_LEN, D)
    input_grad = grads.reshape(SLOTS, SLOT_LEN, D)
    return (output, input_grad) + tuple(totals)
```

```python
import functools

import jax
import jax.numpy as jnp
from jax import lax
from jax.experimental import pallas as pl
from jax.experimental.pallas import tpu as pltpu
from jax.sharding import PartitionSpec as P

HEADS = 8
EPS = 1e-05
NEG = -1e30
AXES = ("dp", "fsdp")
WIDTH = 512
UNIT = 64
TILE = 256
FFC = 512
VMEM_BYTES = 60 * 1024 * 1024
F32 = jnp.float32
BF16 = jnp.bfloat16


def dot_nn(a, b):
    return lax.dot_general(a, b, (((1,), (0,)), ((), ())), preferred_element_type=F32)


def dot_nt(a, b):
    return lax.dot_general(a, b, (((1,), (1,)), ((), ())), preferred_element_type=F32)


def dot_tn(a, b):
    return lax.dot_general(a, b, (((0,), (0,)), ((), ())), preferred_element_type=F32)


def rows_at(start, size, step=UNIT):
    return pl.ds(pl.multiple_of(start, step), size)


def slot_plan(len_ref, val_ref, slots):
    counts, bases, total = [], [], jnp.int32(0)
    for s in range(slots):
        n = jnp.where(val_ref[s] > 0, (len_ref[s] + (UNIT - 1)) // UNIT, 0)
        counts.append(n)
        bases.append(total)
        total = total + n
    return counts, bases, total


def norm_stats(v):
    mean = jnp.mean(v, axis=-1, keepdims=True)
    c = v - mean
    r = lax.rsqrt(jnp.mean(c * c, axis=-1, keepdims=True) + EPS)
    return c * r, r


def pack_body(len_ref, val_ref, cot_ref, ab_ref, cp_ref, ssum_ref, asum_ref):
    slots, length, _ = cot_ref.shape
    counts, bases, _ = slot_plan(len_ref, val_ref, slots)
    cp_ref[...] = jnp.zeros_like(cp_ref)
    ab_t = ab_ref[...].astype(F32).T
    asum = jnp.zeros((1, WIDTH), F32)
    pos = lax.broadcasted_iota(jnp.int32, (length, 1), 0)
    upos = lax.broadcasted_iota(jnp.int32, (UNIT, 1), 0)
    for s in range(slots):
        live = jnp.where(val_ref[s] > 0, len_ref[s], 0)

        def copy(j, _, s=s, live=live):
            v = cot_ref[s, rows_at(j * UNIT, UNIT), :].astype(F32)
            v = jnp.where(upos + j * UNIT < live, v, 0.0)
            cp_ref[rows_at((bases[s] + j) * UNIT, UNIT), :] = v.astype(BF16)
            return 0

        lax.fori_loop(0, counts[s], copy, 0)
        rest = jnp.where(pos >= live, cot_ref[s].astype(F32), 0.0)
        ssum_ref[s : s + 1, :] = jnp.sum(rest, axis=0, keepdims=True)
        asum = asum + jnp.sum(rest * ab_t[:, s : s + 1], axis=0, keepdims=True)
    asum_ref[...] = jnp.broadcast_to(asum, asum_ref.shape)


def device_of(q, me):
    return jnp.bitwise_xor(((q & 15) << 1) | (q >> 4), me)


def place_of(d, me):
    p = jnp.bitwise_xor(d, me)
    return (p & 1) * 16 + (p >> 1)


def lane_pick(first, period, rows=256):
    c = lax.broadcasted_iota(jnp.int32, (rows, WIDTH), 0)
    lane = lax.broadcasted_iota(jnp.int32, (rows, WIDTH), 1)
    return jnp.where(c == first + (lane & (period - 1)), 1.0, 0.0).astype(BF16)


def lane_owner(shift, offset=0):
    d = lax.broadcasted_iota(jnp.int32, (32, WIDTH), 0)
    lane = lax.broadcasted_iota(jnp.int32, (32, WIDTH), 1)
    return ((lane + offset) >> shift) == d


def load_qkv(me, own_ref, rec_ref, w_ref):
    for q in range(32):
        d = device_of(jnp.int32(q), me)
        src = own_ref if q < 16 else rec_ref
        for cb in range(3):
            w_ref[rows_at(d * 16, 16, 16), cb * WIDTH : (cb + 1) * WIDTH] = src[
                q & 15, cb * 16 : (cb + 1) * 16, :
            ]


def attn_fwd_slot(lc, live, s, row0, qkv_ref, mix_ref, lse_ref, ot_ref):
    keep = min(lc, UNIT) if lc < 128 else lc
    span = max(lc, 128)
    rows = rows_at(row0, span)
    v_t = qkv_ref[rows, 2 * WIDTH : 3 * WIDTH].T
    lane = lax.broadcasted_iota(jnp.int32, (span, 128), 1)
    key_row = lax.broadcasted_iota(jnp.int32, (span, span), 0)
    for hp in range(HEADS // 2):
        sl = slice(hp * 128, (hp + 1) * 128)
        q2 = qkv_ref[rows, hp * 128 : (hp + 1) * 128] * BF16(0.125)
        k2 = qkv_ref[rows, WIDTH + hp * 128 : WIDTH + (hp + 1) * 128]
        for half in range(2):
            h = hp * 2 + half
            qm = jnp.where((lane >= 64) == (half == 1), q2, BF16(0))
            sc = dot_nt(k2, qm)
            if lc != 128:
                sc = jnp.where(key_row < live, sc, NEG)
            top = jnp.max(sc, axis=0, keepdims=True)
            ex = jnp.exp(sc - top)
            tot = jnp.sum(ex, axis=0, keepdims=True)
            o = dot_nn(v_t[h * 64 : (h + 1) * 64, :], ex.astype(BF16))
            ot_ref[h * 64 : (h + 1) * 64, 0:span] = (o * (1.0 / tot)).astype(BF16)
            lse_ref[s, h : h + 1, 0:span] = top + jnp.log(tot)
    mix = ot_ref[:, 0:span].T
    mix_ref[rows_at(row0, keep), :] = mix[0:keep]


def by_class(count, fn):
    for n, lc in ((1, 64), (2, 128), (4, 256)):
        pl.when(count == n)(functools.partial(fn, lc))


def front_body(
    me_ref, len_ref, val_ref, step_ref, x_ref, ab_ref, own_ref, rec_ref,
    start_ref, n1_ref, qkv_ref, mix_ref, lse_ref, out_ref, vec_ref,
    w_ref, time_ref, g_ref, abt_ref, ot_ref, cnt_ref, base_ref,
):
    slots, length, _ = x_ref.shape
    me = me_ref[0]
    counts, bases, total = slot_plan(len_ref, val_ref, slots)
    for s in range(slots):
        cnt_ref[s] = counts[s]
        base_ref[s] = bases[s]
    tiles = (total * UNIT + TILE - 1) // TILE
    load_qkv(me, own_ref, rec_ref, w_ref)
    for q in range(32):
        d = device_of(jnp.int32(q), me)
        src = own_ref if q < 16 else rec_ref
        tail = src[q & 15, 48:64, :].astype(F32)
        time_ref[pl.ds(pl.multiple_of(d * 8, 8), 8), :] = tail[0:8]
        g_ref[pl.ds(d, 1), :] = tail[8:9]
    g = g_ref[:, 0:256].astype(BF16)
    own16 = lane_owner(4)
    for v in range(9):
        t = dot_nn(g, lane_pick(16 * v, 16))
        vec_ref[v : v + 1, :] = jnp.sum(jnp.where(own16, t, 0.0), axis=0, keepdims=True)
    t = dot_nn(g, lane_pick(144, 64))
    for c in range(4):
        vec_ref[9 + c : 10 + c, :] = jnp.sum(
            jnp.where(lane_owner(6, c * WIDTH), t, 0.0), axis=0, keepdims=True
        )
    vec_ref[13:16, :] = jnp.zeros((3, WIDTH), F32)
    gain, shift = vec_ref[0:1, :], vec_ref[1:2, :]
    absorb = vec_ref[8:9, :]
    abt_ref[:, 0:slots] = ab_ref[...].astype(F32).T
    n1_ref[...] = jnp.zeros_like(n1_ref)
    start_ref[...] = jnp.zeros_like(start_ref)
    for s in range(slots):
        row = time_ref[pl.ds(step_ref[s], 1), :]

        def unit(j, _, s=s, row=row):
            here = rows_at(j * UNIT, UNIT)
            v = x_ref[s, here, :].astype(F32) + row + abt_ref[here, s : s + 1] * absorb
            out_ref[s, here, :] = v.astype(BF16)

            @pl.when(j < counts[s])
            def _():
                there = rows_at((bases[s] + j) * UNIT, UNIT)
                start_ref[there, :] = v
                u, _r = norm_stats(v)
                n1_ref[there, :] = (u * gain + shift).astype(BF16)

            return 0

        lax.fori_loop(0, length // UNIT, unit, 0)

    def project(t, _):
        here = rows_at(t * TILE, TILE, TILE)
        n1 = n1_ref[here, :]
        for cb in range(3):
            cols = slice(cb * WIDTH, (cb + 1) * WIDTH)
            p = dot_nn(n1, w_ref[:, cols])
            if cb == 0:
                p = p + vec_ref[2:3, :]
            if cb == 2:
                p = p + vec_ref[3:4, :]
            qkv_ref[here, cols] = p.astype(BF16)
        return 0

    lax.fori_loop(0, tiles, project, 0)

    @pl.when(tiles < qkv_ref.shape[0] // TILE)
    def _():
        qkv_ref[rows_at(tiles * TILE, TILE, TILE), :] = jnp.zeros((TILE, 3 * WIDTH), BF16)

    mix_ref[...] = jnp.zeros_like(mix_ref)

    def slot(s, _):
        def run(lc):
            attn_fwd_slot(
                lc, len_ref[s], s, base_ref[s] * UNIT, qkv_ref, mix_ref, lse_ref, ot_ref
            )

        by_class(cnt_ref[s], run)
        return 0

    lax.fori_loop(0, slots, slot, 0)


def load_mlp(me, own_ref, rec_ref, wu_ref, wd_ref, wp_ref):
    for q in range(32):
        d = device_of(jnp.int32(q), me)
        src = own_ref if q < 16 else rec_ref
        for cb in range(4):
            wu_ref[rows_at(d * 16, 16, 16), cb * WIDTH : (cb + 1) * WIDTH] = src[
                q & 15, cb * 16 : (cb + 1) * 16, :
            ]
        wd_ref[rows_at(d * 64, 64, 64), :] = src[q & 15, 64:128, :]
        wp_ref[rows_at(d * 16, 16, 16), :] = src[q & 15, 128:144, :]


def gelu_pair(x):
    c0 = 0.7978845608028654
    x2 = x * x
    t = jnp.tanh(x * (c0 + (c0 * 0.044715) * x2))
    half = 0.5 + 0.5 * t
    slope = half + (0.5 * x) * (1.0 - t * t) * (c0 + (3.0 * 0.044715 * c0) * x2)
    return x * half, slope


def mlp_body(
    me_ref, len_ref, val_ref, mix_ref, start_ref, cp_ref, vec_ref, out0_ref, own_ref, rec_ref,
    out_ref, gmid_ref, gmix_ref, keep_ref, send_ref, vg_ref,
    wu_ref, wd_ref, wp_ref, mid_ref, n2_ref, y_ref, g2_ref, act_ref, gh_ref, dwu_ref, dwd_ref, gub_ref,
):
    slots = out_ref.shape[0]
    me = me_ref[0]
    counts, bases, total = slot_plan(len_ref, val_ref, slots)
    tiles = (total * UNIT + TILE - 1) // TILE
    pairs = (tiles + 1) // 2
    load_mlp(me, own_ref, rec_ref, wu_ref, wd_ref, wp_ref)
    gain, shift = vec_ref[5:6, :], vec_ref[6:7, :]

    def mask_of(t):
        r = lax.broadcasted_iota(jnp.int32, (TILE, 1), 0) + t * TILE
        ok = r < total * UNIT
        for s in range(slots):
            bad = (r >= bases[s] * UNIT + len_ref[s]) & (r < (bases[s] + counts[s]) * UNIT)
            ok = ok & jnp.logical_not(bad)
        return jnp.where(ok, 1.0, 0.0)

    def first(t, _):
        here = rows_at(t * TILE, TILE, TILE)
        att = dot_nn(mix_ref[here, :], wp_ref[...]) + vec_ref[4:5, :]
        mid = start_ref[here, :] + mask_of(t) * att
        mid_ref[here, :] = mid
        u, _r = norm_stats(mid)
        n2_ref[here, :] = (u * gain + shift).astype(BF16)
        return 0

    lax.fori_loop(0, tiles, first, 0)

    @pl.when(tiles % 2 == 1)
    def _():
        here = rows_at(tiles * TILE, TILE, TILE)
        act_ref[here, :] = jnp.zeros((TILE, FFC), BF16)
        gh_ref[here, :] = jnp.zeros((TILE, FFC), BF16)
        n2_ref[here, :] = jnp.zeros((TILE, WIDTH), BF16)
        gmid_ref[here, :] = jnp.zeros((TILE, WIDTH), F32)

    for c in range(4):
        cols = slice(c * FFC, (c + 1) * FFC)
        bias = vec_ref[9 + c : 10 + c, :]
        gub_ref[...] = jnp.zeros_like(gub_ref)

        def step(t, _, c=c, cols=cols, bias=bias):
            here = rows_at(t * TILE, TILE, TILE)
            h = dot_nn(n2_ref[here, :], wu_ref[:, cols]) + bias
            ga = dot_nt(cp_ref[here, :], wd_ref[cols, :])
            act, slope = gelu_pair(h)
            gh = ga * slope
            act = act.astype(BF16)
            gh = gh.astype(BF16)
            act_ref[here, :] = act
            gh_ref[here, :] = gh
            gub_ref[...] += jnp.sum(gh.astype(F32).reshape(TILE // 8, 8, FFC), axis=0)
            y = dot_nn(act, wd_ref[cols, :])
            g2 = dot_nt(gh, wu_ref[:, cols])
            if c == 0:
                y_ref[here, :] = y
                g2_ref[here, :] = g2
            else:
                y_ref[here, :] += y
                g2_ref[here, :] += g2
            return 0

        lax.fori_loop(0, tiles, step, 0)
        dwu_ref[...] = jnp.zeros_like(dwu_ref)
        dwd_ref[...] = jnp.zeros_like(dwd_ref)

        def weights(k, _):
            here = rows_at(k * 2 * TILE, 2 * TILE, 2 * TILE)
            dwu_ref[...] += dot_tn(n2_ref[here, :], gh_ref[here, :])
            dwd_ref[...] += dot_tn(act_ref[here, :], cp_ref[here, :])
            return 0

        lax.fori_loop(0, pairs, weights, 0)
        vg_ref[9 + c : 10 + c, :] = jnp.sum(gub_ref[...], axis=0, keepdims=True)
        for q in range(32):
            d = device_of(jnp.int32(q), me)
            dst = keep_ref if q < 16 else send_ref
            dst[q & 15, c * 16 : (c + 1) * 16, :] = dwu_ref[rows_at(d * 16, 16, 16), :].astype(BF16)
        for i in range(8):
            d = jnp.int32(8 * c + i)
            piece = dwd_ref[i * 64 : (i + 1) * 64, :].astype(BF16)
            place = place_of(d, me)
            pl.when(place < 16)(
                functools.partial(keep_ref.__setitem__, (place & 15, slice(64, 128)), piece)
            )
            pl.when(place >= 16)(
                functools.partial(send_ref.__setitem__, (place & 15, slice(64, 128)), piece)
            )

    vg_ref[0:9, :] = jnp.zeros((9, WIDTH), F32)
    vg_ref[13:16, :] = jnp.zeros((3, WIDTH), F32)

    def last(t, _):
        here = rows_at(t * TILE, TILE, TILE)
        mid = mid_ref[here, :]
        u, r = norm_stats(mid)
        y_ref[here, :] = mid + (y_ref[here, :] + vec_ref[7:8, :])
        g2 = g2_ref[here, :]
        e = g2 * gain
        cot = cp_ref[here, :].astype(F32)
        gm = cot + r * (
            e - jnp.mean(e, axis=-1, keepdims=True) - u * jnp.mean(e * u, axis=-1, keepdims=True)
        )
        gmid_ref[here, :] = gm
        ga = gm.astype(BF16)
        gmix_ref[here, :] = dot_nt(ga, wp_ref[...]).astype(BF16)
        vg_ref[5:6, :] += jnp.sum(g2 * u, axis=0, keepdims=True)
        vg_ref[6:7, :] += jnp.sum(g2, axis=0, keepdims=True)
        vg_ref[7:8, :] += jnp.sum(cot, axis=0, keepdims=True)
        vg_ref[4:5, :] += jnp.sum(ga.astype(F32), axis=0, keepdims=True)
        return 0

    lax.fori_loop(0, tiles, last, 0)
    dwu_ref[...] = jnp.zeros_like(dwu_ref)

    def proj(k, _):
        here = rows_at(k * 2 * TILE, 2 * TILE, 2 * TILE)
        dwu_ref[...] += dot_tn(mix_ref[here, :], gmid_ref[here, :].astype(BF16))
        return 0

    lax.fori_loop(0, pairs, proj, 0)
    for q in range(32):
        d = device_of(jnp.int32(q), me)
        dst = keep_ref if q < 16 else send_ref
        dst[q & 15, 128:144, :] = dwu_ref[rows_at(d * 16, 16, 16), :].astype(BF16)

    upos = lax.broadcasted_iota(jnp.int32, (UNIT, 1), 0)
    for s in range(slots):

        def spread(j, _, s=s):
            here = rows_at(j * UNIT, UNIT)

            @pl.when(j < counts[s])
            def _():
                new = y_ref[rows_at((bases[s] + j) * UNIT, UNIT), :].astype(BF16).astype(F32)
                old = out0_ref[s, here, :].astype(F32)
                out_ref[s, here, :] = jnp.where(upos + j * UNIT < len_ref[s], new, old).astype(BF16)

            @pl.when(j >= counts[s])
            def _():
                out_ref[s, here, :] = out0_ref[s, here, :]

            return 0

        lax.fori_loop(0, out_ref.shape[1] // UNIT, spread, 0)


def attn_bwd_slot(lc, live, s, row0, qkv_ref, lse_ref, gmix_ref, gpi_ref, ot_ref):
    keep = min(lc, UNIT) if lc < 128 else lc
    span = max(lc, 128)
    rows = rows_at(row0, span)
    out_rows = rows_at(row0, keep)
    k_t = qkv_ref[rows, WIDTH : 2 * WIDTH].T
    lane = lax.broadcasted_iota(jnp.int32, (span, 128), 1)
    key_row = lax.broadcasted_iota(jnp.int32, (span, span), 0)
    query_col = lax.broadcasted_iota(jnp.int32, (span, span), 1)
    for hp in range(HEADS // 2):
        q2 = qkv_ref[rows, hp * 128 : (hp + 1) * 128] * BF16(0.125)
        k2 = qkv_ref[rows, WIDTH + hp * 128 : WIDTH + (hp + 1) * 128]
        v2 = qkv_ref[rows, 2 * WIDTH + hp * 128 : 2 * WIDTH + (hp + 1) * 128]
        o2 = gmix_ref[rows, hp * 128 : (hp + 1) * 128]
        gk, gv = None, None
        for half in range(2):
            h = hp * 2 + half
            here = (lane >= 64) == (half == 1)
            qm = jnp.where(here, q2, BF16(0))
            om = jnp.where(here, o2, BF16(0))
            sc = dot_nt(k2, qm)
            p = jnp.exp(sc - lse_ref[s, h : h + 1, 0:span])
            if lc != 128:
                ok = key_row < live
                if lc < 128:
                    ok = ok & (query_col < live)
                p = jnp.where(ok, p, 0.0)
            dp = dot_nt(v2, om)
            row = jnp.sum(p * dp, axis=0, keepdims=True)
            ds = (p * (dp - row)).astype(BF16)
            ot_ref[h * 64 : (h + 1) * 64, 0:span] = (
                dot_nn(k_t[h * 64 : (h + 1) * 64, :], ds) * 0.125
            ).astype(BF16)
            a = dot_nn(ds, qm)
            b = dot_nn(p.astype(BF16), om)
            gk = a if gk is None else gk + a
            gv = b if gv is None else gv + b
        gpi_ref[out_rows, WIDTH + hp * 128 : WIDTH + (hp + 1) * 128] = gk[0:keep].astype(BF16)
        gpi_ref[out_rows, 2 * WIDTH + hp * 128 : 2 * WIDTH + (hp + 1) * 128] = gv[0:keep].astype(
            BF16
        )
    gpi_ref[out_rows, 0:WIDTH] = ot_ref[:, 0:span].T[0:keep]


def back_body(
    me_ref, len_ref, val_ref, step_ref, qkv_ref, lse_ref, gmix_ref, n1_ref, start_ref, gmid_ref,
    cot_ref, ab_ref, vec_ref, vgin_ref, ssum_ref, asum_ref, own_ref, rec_ref,
    ig_ref, keep_ref, send_ref,
    w_ref, gpi_ref, dw_ref, vg_ref, tg_ref, slot_ref, abt_ref, ot_ref, gout_ref, cnt_ref, base_ref,
):
    slots = ig_ref.shape[0]
    me = me_ref[0]
    counts, bases, total = slot_plan(len_ref, val_ref, slots)
    for s in range(slots):
        cnt_ref[s] = counts[s]
        base_ref[s] = bases[s]
    tiles = (total * UNIT + TILE - 1) // TILE
    pairs = (tiles + 1) // 2
    load_qkv(me, own_ref, rec_ref, w_ref)
    gpi_ref[...] = jnp.zeros_like(gpi_ref)

    def slot(s, _):
        def run(lc):
            attn_bwd_slot(
                lc, len_ref[s], s, base_ref[s] * UNIT, qkv_ref, lse_ref, gmix_ref, gpi_ref, ot_ref
            )

        by_class(cnt_ref[s], run)
        return 0

    lax.fori_loop(0, slots, slot, 0)

    vg_ref[...] = vgin_ref[...]
    gain = vec_ref[0:1, :]
    dw_ref[...] = jnp.zeros_like(dw_ref)

    def weights(k, _):
        here = rows_at(k * 2 * TILE, 2 * TILE, 2 * TILE)
        n1 = n1_ref[here, :]
        for cb in range(3):
            cols = slice(cb * WIDTH, (cb + 1) * WIDTH)
            g = gpi_ref[here, cols]
            dw_ref[:, cols] += dot_tn(n1, g)
            if cb == 0:
                vg_ref[2:3, :] += jnp.sum(g.astype(F32), axis=0, keepdims=True)
            if cb == 2:
                vg_ref[3:4, :] += jnp.sum(g.astype(F32), axis=0, keepdims=True)
        return 0

    lax.fori_loop(0, pairs, weights, 0)

    def norm(t, _):
        here = rows_at(t * TILE, TILE, TILE)
        g1 = dot_nt(gpi_ref[here, :], w_ref[...])
        u, r = norm_stats(start_ref[here, :])
        e = g1 * gain
        gmid_ref[here, :] += r * (
            e - jnp.mean(e, axis=-1, keepdims=True) - u * jnp.mean(e * u, axis=-1, keepdims=True)
        )
        vg_ref[0:1, :] += jnp.sum(g1 * u, axis=0, keepdims=True)
        vg_ref[1:2, :] += jnp.sum(g1, axis=0, keepdims=True)
        return 0

    lax.fori_loop(0, tiles, norm, 0)

    abt_ref[:, 0:slots] = ab_ref[...].astype(F32).T
    vg_ref[8:9, :] = asum_ref[0:1, :]
    slot_ref[...] = ssum_ref[...]
    upos = lax.broadcasted_iota(jnp.int32, (UNIT, 1), 0)
    for s in range(slots):

        def spread(j, _, s=s):
            here = rows_at(j * UNIT, UNIT)

            @pl.when(j < counts[s])
            def _():
                new = gmid_ref[rows_at((bases[s] + j) * UNIT, UNIT), :]
                old = cot_ref[s, here, :].astype(F32)
                ig_ref[s, here, :] = jnp.where(upos + j * UNIT < len_ref[s], new, old).astype(BF16)
                slot_ref[s : s + 1, :] += jnp.sum(new, axis=0, keepdims=True)
                vg_ref[8:9, :] += jnp.sum(new * abt_ref[here, s : s + 1], axis=0, keepdims=True)

            @pl.when(j >= counts[s])
            def _():
                ig_ref[s, here, :] = cot_ref[s, here, :]

            return 0

        lax.fori_loop(0, ig_ref.shape[1] // UNIT, spread, 0)

    tg_ref[...] = jnp.zeros_like(tg_ref)
    for s in range(slots):
        tg_ref[pl.ds(step_ref[s], 1), :] += slot_ref[s : s + 1, :]

    own16 = lane_owner(4)
    gout = jnp.zeros((32, 256), F32)
    for v in range(9):
        row = jnp.broadcast_to(vg_ref[v : v + 1, :], (32, WIDTH))
        gout = gout + dot_nt(jnp.where(own16, row, 0.0).astype(BF16), lane_pick(16 * v, 16))
    wide = jnp.zeros((32, WIDTH), F32)
    for c in range(4):
        row = jnp.broadcast_to(vg_ref[9 + c : 10 + c, :], (32, WIDTH))
        wide = wide + jnp.where(lane_owner(6, c * WIDTH), row, 0.0)
    gout = gout + dot_nt(wide.astype(BF16), lane_pick(144, 64))
    gout_ref[:, 0:256] = gout
    gout_ref[:, 256:512] = jnp.zeros((32, 256), F32)
    for q in range(32):
        d = device_of(jnp.int32(q), me)
        dst = keep_ref if q < 16 else send_ref
        for cb in range(3):
            dst[q & 15, cb * 16 : (cb + 1) * 16, :] = dw_ref[
                rows_at(d * 16, 16, 16), cb * WIDTH : (cb + 1) * WIDTH
            ].astype(BF16)
        t = tg_ref[pl.ds(pl.multiple_of(d * 8, 8), 8), :]
        v = jnp.broadcast_to(gout_ref[pl.ds(d, 1), :], (8, WIDTH))
        dst[q & 15, 48:64, :] = jnp.concatenate([t, v], axis=0).astype(BF16)


SMEM = pl.BlockSpec(memory_space=pltpu.SMEM)
VMEM = pl.BlockSpec(memory_space=pltpu.VMEM)


def call(body, outs, scratch, n_smem, *args):
    return pl.pallas_call(
        body,
        out_shape=[jax.ShapeDtypeStruct(s, d) for s, d in outs],
        in_specs=[SMEM] * n_smem + [VMEM] * (len(args) - n_smem),
        out_specs=[VMEM] * len(outs),
        scratch_shapes=scratch,
        compiler_params=pltpu.CompilerParams(vmem_limit_bytes=VMEM_BYTES),
    )(*args)


def pack_rows(lengths, validity, cotangent, absorbed):
    slots, length, width = cotangent.shape
    return call(
        pack_body,
        [((slots * length, width), BF16), ((slots, width), F32), ((8, width), F32)],
        [],
        2,
        lengths, validity, cotangent, absorbed,
    )


def front(me, lengths, validity, timesteps, inputs, absorbed, own, rec, t_rows):
    slots, length, width = inputs.shape
    rows = slots * length
    return call(
        front_body,
        [
            ((rows, width), F32),
            ((rows, width), BF16),
            ((rows, 3 * width), BF16),
            ((rows, width), BF16),
            ((slots, HEADS, length), F32),
            ((slots, length, width), BF16),
            ((16, width), F32),
        ],
        [
            pltpu.VMEM((width, 3 * width), BF16),
            pltpu.VMEM((t_rows, width), F32),
            pltpu.VMEM((32, width), F32),
            pltpu.VMEM((length, 128), F32),
            pltpu.VMEM((width, length), BF16),
            pltpu.SMEM((slots,), jnp.int32),
            pltpu.SMEM((slots,), jnp.int32),
        ],
        4,
        me, lengths, validity, timesteps, inputs, absorbed, own, rec,
    )


def mlp(me, lengths, validity, mix, start, cp, vec, out0, own, rec):
    slots, length, width = out0.shape
    rows = slots * length
    ff = 4 * FFC
    return call(
        mlp_body,
        [
            ((slots, length, width), BF16),
            ((rows, width), F32),
            ((rows, width), BF16),
            ((16, 144, width), BF16),
            ((16, 144, width), BF16),
            ((16, width), F32),
        ],
        [
            pltpu.VMEM((width, ff), BF16),
            pltpu.VMEM((ff, width), BF16),
            pltpu.VMEM((width, width), BF16),
            pltpu.VMEM((rows, width), F32),
            pltpu.VMEM((rows, width), BF16),
            pltpu.VMEM((rows, width), F32),
            pltpu.VMEM((rows, width), F32),
            pltpu.VMEM((rows, FFC), BF16),
            pltpu.VMEM((rows, FFC), BF16),
            pltpu.VMEM((width, FFC), F32),
            pltpu.VMEM((FFC, width), F32),
            pltpu.VMEM((8, FFC), F32),
        ],
        3,
        me, lengths, validity, mix, start, cp, vec, out0, own, rec,
    )


def back(
    me, lengths, validity, timesteps, qkv, lse, gmix, n1, start, gmid, cot, absorbed, vec, vg,
    ssum, asum, own, rec, t_rows,
):
    slots, length, width = cot.shape
    rows = slots * length
    return call(
        back_body,
        [
            ((slots, length, width), BF16),
            ((16, 64, width), BF16),
            ((16, 64, width), BF16),
        ],
        [
            pltpu.VMEM((width, 3 * width), BF16),
            pltpu.VMEM((rows, 3 * width), BF16),
            pltpu.VMEM((width, 3 * width), F32),
            pltpu.VMEM((16, width), F32),
            pltpu.VMEM((t_rows, width), F32),
            pltpu.VMEM((slots, width), F32),
            pltpu.VMEM((length, 128), F32),
            pltpu.VMEM((width, length), BF16),
            pltpu.VMEM((32, width), F32),
            pltpu.SMEM((slots,), jnp.int32),
            pltpu.SMEM((slots,), jnp.int32),
        ],
        4,
        me, lengths, validity, timesteps, qkv, lse, gmix, n1, start, gmid, cot, absorbed, vec, vg,
        ssum, asum, own, rec,
    )


def hop(x, mask):
    return lax.ppermute(x, AXES, [(i, i ^ mask) for i in range(32)])


def spread_blocks(x):
    b = jnp.stack([x] + [hop(x, m) for m in (2, 4, 6)])
    b = jnp.concatenate([b] + [hop(b, m) for m in (8, 16, 24)])
    return b, hop(b, 1)


def gather_any(x, n):
    g = lax.all_gather(x, AXES, axis=0, tiled=False)
    return g


def add_up(*parts):
    total = parts[0].astype(F32)
    for p in parts[1:]:
        total = total + p.astype(F32)
    return total


def reduce_blocks(keep, send):
    s = add_up(keep, hop(send, 1)).astype(BF16)
    s = add_up(s[0:4], *[hop(s[4 * k : 4 * k + 4], 8 * k) for k in (1, 2, 3)]).astype(BF16)
    return add_up(s[0], *[hop(s[k], 2 * k) for k in (1, 2, 3)])


def column_blocks(w):
    rows, cols = w.shape
    return [w[:, c : c + WIDTH] for c in range(0, cols, WIDTH)]


def shards(
    n_dev,
    inputs,
    lengths,
    validity,
    absorbed,
    timesteps,
    attn_gain,
    attn_shift,
    query_key_value_weight,
    query_bias,
    value_bias,
    output_projection_weight,
    output_projection_bias,
    mlp_gain,
    mlp_shift,
    up_projection_weight,
    hidden_units_bias,
    down_projection_weight,
    down_output_bias,
    absorb_vector,
    time_table,
    cotangent,
):
    t_rows = time_table.shape[0] * n_dev
    vectors = [
        attn_gain, attn_shift, query_bias, value_bias, output_projection_bias,
        mlp_gain, mlp_shift, down_output_bias, absorb_vector, hidden_units_bias,
    ]
    weights1 = (query_key_value_weight, time_table)
    weights2 = (up_projection_weight, down_projection_weight, output_projection_weight)

    def first_block(qkv, time, vecs):
        row = jnp.concatenate(vecs)
        row = jnp.pad(row, (0, WIDTH - row.shape[0]))
        tail = jnp.concatenate([time, jnp.broadcast_to(row[None], (8, WIDTH))])
        return jnp.concatenate(column_blocks(qkv) + [tail])

    def second_block(up, down, proj):
        return jnp.concatenate(column_blocks(up) + [down, proj])

    if n_dev == 32:
        me = lax.axis_index(AXES).astype(jnp.int32)
        own1, rec1 = spread_blocks(first_block(*weights1, vectors))
        own2, rec2 = spread_blocks(second_block(*weights2))
    else:
        me = jnp.int32(0)

        def whole(x):
            full = lax.all_gather(x, AXES, axis=0, tiled=True)
            return full.reshape((32, full.shape[0] // 32) + full.shape[1:])

        b1 = jax.vmap(first_block)(*[whole(w) for w in weights1], [whole(v) for v in vectors])
        b2 = jax.vmap(second_block)(*[whole(w) for w in weights2])
        own1, rec1, own2, rec2 = b1[0::2], b1[1::2], b2[0::2], b2[1::2]
    me = me.reshape(1)
    cp, ssum, asum = pack_rows(lengths, validity, cotangent, absorbed)
    start, n1, qkv, mix, lse, out0, vec = front(
        me, lengths, validity, timesteps, inputs, absorbed, own1, rec1, t_rows
    )
    output, gmid, gmix, keep2, send2, vg = mlp(
        me, lengths, validity, mix, start, cp, vec, out0, own2, rec2
    )
    input_grad, keep1, send1 = back(
        me, lengths, validity, timesteps, qkv, lse, gmix, n1, start, gmid, cotangent, absorbed,
        vec, vg, ssum, asum, own1, rec1, t_rows,
    )
    if n_dev == 32:
        g2 = reduce_blocks(keep2, send2)[None]
        g1 = reduce_blocks(keep1, send1)[None]
    else:
        g2 = jnp.stack([keep2, send2], 1).reshape((32,) + keep2.shape[1:]).astype(F32)
        g1 = jnp.stack([keep1, send1], 1).reshape((32,) + keep1.shape[1:]).astype(F32)

    def columns(g, lo, n):
        return jnp.concatenate([g[:, lo + 16 * c : lo + 16 * c + 16] for c in range(n)], axis=2)

    row = g1[:, 56]
    small = [row[:, 16 * v : 16 * v + 16] for v in range(9)] + [row[:, 144:208]]
    grads = [
        small[0], small[1], columns(g1, 0, 3), small[2], small[3], g2[:, 128:144], small[4],
        small[5], small[6], columns(g2, 0, 4), small[9], g2[:, 64:128], small[7], small[8],
        g1[:, 48:56],
    ]
    grads = [g.reshape((-1,) + g.shape[2:]) for g in grads]
    if n_dev != 32:
        grads = [lax.psum_scatter(g, AXES, scatter_dimension=0, tiled=True) for g in grads]
    return (output, input_grad) + tuple(grads)


def solution(mesh):
    lead = P(AXES)
    n_dev = mesh.shape["dp"] * mesh.shape["fsdp"]
    return jax.shard_map(
        functools.partial(shards, n_dev),
        mesh=mesh,
        in_specs=(lead,) * 21,
        out_specs=(lead,) * 17,
        check_vma=False,
    )
```

```python
import functools

import jax
import jax.numpy as jnp
from jax import lax
from jax.experimental import pallas as pl
from jax.experimental.pallas import tpu as pltpu
from jax.sharding import PartitionSpec as P

HEADS = 8
EPS = 1e-05
NEG = -1e30
AXES = ("dp", "fsdp")
WIDTH = 512
FF = 2048
UNIT = 64
TILE = 256
PAIR = 2 * TILE
FFC = 512
ROWS1 = 64
ROWS2 = 144
VMEM_BYTES = 60 * 1024 * 1024
F32 = jnp.float32
BF16 = jnp.bfloat16


def dot_nn(a, b):
    return lax.dot_general(a, b, (((1,), (0,)), ((), ())), preferred_element_type=F32)


def dot_nt(a, b):
    return lax.dot_general(a, b, (((1,), (1,)), ((), ())), preferred_element_type=F32)


def dot_tn(a, b):
    return lax.dot_general(a, b, (((0,), (0,)), ((), ())), preferred_element_type=F32)


def rows_at(start, size, step=UNIT):
    return pl.ds(pl.multiple_of(start, step), size)


def tile_at(t, size=TILE):
    return rows_at(t * size, size, size)


def slot_plan(len_ref, val_ref, cnt_ref, base_ref):
    total = jnp.int32(0)
    for s in range(len_ref.shape[0]):
        n = jnp.where(val_ref[s] > 0, (len_ref[s] + (UNIT - 1)) // UNIT, 0)
        cnt_ref[s] = n
        base_ref[s] = total
        total = total + n
    return total, (total * UNIT + TILE - 1) // TILE


def by_class(count, fn):
    for n in (1, 2, 4):
        pl.when(count == n)(functools.partial(fn, n))


def norm_stats(v):
    mean = jnp.mean(v, axis=-1, keepdims=True)
    c = v - mean
    r = lax.rsqrt(jnp.mean(c * c, axis=-1, keepdims=True) + EPS)
    return c * r, r


def norm_back(grad, u, r, gain):
    e = grad * gain
    return r * (
        e - jnp.mean(e, axis=-1, keepdims=True) - u * jnp.mean(e * u, axis=-1, keepdims=True)
    )


def fold8(v):
    return jnp.sum(v.reshape(v.shape[0] // 8, 8, v.shape[1]), axis=0)


def copies(src, dst, sem, t):
    return pltpu.make_async_copy(src.at[tile_at(t)], dst.at[tile_at(t)], sem.at[t])


def start_tiles(tiles, *triples):
    for t in range(8):

        @pl.when(t < tiles)
        def _(t=t):
            for src, dst, sem in triples:
                copies(src, dst, sem, t).start()


def wait_tiles(tiles, *triples):
    for t in range(8):

        @pl.when(t < tiles)
        def _(t=t):
            for src, dst, sem in triples:
                copies(src, dst, sem, t).wait()


def device_of(q, me):
    return jnp.bitwise_xor(((q & 15) << 1) | (q >> 4), me)


def place_of(d, me):
    p = jnp.bitwise_xor(d, me)
    return (p & 1) * 16 + (p >> 1)


def block_body(*refs):
    qkv, time, up, down, proj = refs[:5]
    vecs = refs[5:15]
    one_ref, two_ref, tail_ref = refs[15:]
    for c in range(3):
        one_ref[c * 16 : (c + 1) * 16, :] = qkv[:, c * WIDTH : (c + 1) * WIDTH]
    tail_ref[...] = jnp.zeros_like(tail_ref)
    tail_ref[0:8, :] = time[...].astype(F32)
    for v in range(8):
        tail_ref[8 + v : 9 + v, 0:16] = vecs[v][...].astype(F32)
    tail_ref[8:9, 128:144] = vecs[8][...].astype(F32)
    tail_ref[8:9, 256:320] = vecs[9][...].astype(F32)
    one_ref[48:64, :] = tail_ref[...].astype(BF16)
    for c in range(4):
        two_ref[c * 16 : (c + 1) * 16, :] = up[:, c * WIDTH : (c + 1) * WIDTH]
    two_ref[64:128, :] = down[...]
    two_ref[128:144, :] = proj[...]


def join_body(a, b, c, d, o):
    o[0], o[1], o[2], o[3] = a[...], b[...], c[...], d[...]


def pack_body(len_ref, val_ref, cot_ref, ab_ref, cp_ref, ig_ref, ssum_ref, asum_ref, cnt_ref, base_ref):
    slots, length, _ = cot_ref.shape
    total, tiles = slot_plan(len_ref, val_ref, cnt_ref, base_ref)

    def clear(u, _):
        cp_ref[rows_at(u * UNIT, UNIT), :] = jnp.zeros((UNIT, WIDTH), BF16)
        return 0

    lax.fori_loop(total, tiles * (TILE // UNIT), clear, 0)
    pl.when(tiles % 2 == 1)(
        lambda: cp_ref.__setitem__((tile_at(tiles), slice(None)), jnp.zeros((TILE, WIDTH), BF16))
    )
    ab_t = ab_ref[...].astype(F32).T
    asum = jnp.zeros((8, WIDTH), F32)
    pos = lax.broadcasted_iota(jnp.int32, (length, 1), 0)
    for s in range(slots):
        live = jnp.where(val_ref[s] > 0, len_ref[s], 0)
        raw = cot_ref[s]
        ig_ref[s] = raw
        v = raw.astype(F32)
        ok = pos < live

        def put(n, s=s, v=v, ok=ok):
            size = n * UNIT
            cp_ref[rows_at(base_ref[s] * UNIT, size), :] = jnp.where(ok, v, 0.0)[0:size].astype(BF16)

        by_class(cnt_ref[s], put)
        rest = jnp.where(ok, 0.0, v)
        ssum_ref[s : s + 1, :] = jnp.sum(rest, axis=0, keepdims=True)
        asum = asum + fold8(rest * ab_t[:, s : s + 1])
    asum_ref[...] = asum


def load_qkv(me, blocks, w_ref):
    for q in range(32):
        d = device_of(jnp.int32(q), me)
        for c in range(3):
            w_ref[rows_at(d * 16, 16, 16), c * WIDTH : (c + 1) * WIDTH] = blocks[q >> 2][
                q & 3, c * 16 : (c + 1) * 16, :
            ]


def attn_fwd_slot(n, live, s, row0, qkv_ref, mix_ref, lse_ref, ot_ref):
    keep = n * UNIT
    span = max(keep, 128)
    rows = rows_at(row0, span)
    v_t = qkv_ref[rows, 2 * WIDTH : 3 * WIDTH].T
    lane = lax.broadcasted_iota(jnp.int32, (span, 128), 1)
    key_row = lax.broadcasted_iota(jnp.int32, (span, span), 0)
    for hp in range(HEADS // 2):
        q2 = qkv_ref[rows, hp * 128 : (hp + 1) * 128] * BF16(0.125)
        k2 = qkv_ref[rows, WIDTH + hp * 128 : WIDTH + (hp + 1) * 128]
        for half in range(2):
            h = hp * 2 + half
            qm = jnp.where((lane >= 64) == (half == 1), q2, BF16(0))
            sc = dot_nt(k2, qm)
            if n != 2:
                sc = jnp.where(key_row < live, sc, NEG)
            top = jnp.max(sc, axis=0, keepdims=True)
            ex = jnp.exp(sc - top)
            tot = jnp.sum(ex, axis=0, keepdims=True)
            o = dot_nn(v_t[h * 64 : (h + 1) * 64, :], ex.astype(BF16))
            ot_ref[h * 64 : (h + 1) * 64, 0:span] = (o * (1.0 / tot)).astype(BF16)
            lse_ref[s, h : h + 1, 0:span] = top + jnp.log(tot)
    mix_ref[rows_at(row0, keep), :] = ot_ref[:, 0:span].T[0:keep]


def front_body(
    me_ref, len_ref, val_ref, step_ref, ab_ref, x_hbm, b0, b1, b2, b3, b4, b5, b6, b7,
    start_hbm, n1_hbm, qkv_hbm, mix_hbm, lse_ref, out_hbm, vec_ref,
    x_ref, start_ref, n1_ref, qkv_ref, mix_ref, out_ref, w_ref, time_ref, ot_ref,
    cnt_ref, base_ref, sem_x, sem_s, sem_n, sem_q, sem_m, sem_o,
):
    slots, length, _ = x_ref.shape
    blocks = (b0, b1, b2, b3, b4, b5, b6, b7)
    me = me_ref[0]
    for s in range(slots):
        pltpu.make_async_copy(x_hbm.at[s], x_ref.at[s], sem_x.at[s]).start()
    total, tiles = slot_plan(len_ref, val_ref, cnt_ref, base_ref)
    load_qkv(me, blocks, w_ref)
    lane = lax.broadcasted_iota(jnp.int32, (8, WIDTH), 1)
    row8 = lax.broadcasted_iota(jnp.int32, (8, WIDTH), 0)
    short = jnp.zeros((8, WIDTH), F32)
    gone = jnp.zeros((8, WIDTH), F32)
    vec_ref[...] = jnp.zeros_like(vec_ref)
    for q in range(32):
        d = device_of(jnp.int32(q), me)
        tail = blocks[q >> 2][q & 3, 48:64, :].astype(F32)
        time_ref[rows_at(d * 8, 8, 8), :] = tail[0:8]
        t = tail[8:16]
        short = short + pltpu.roll(jnp.where(lane < 16, t, 0.0), d * 16, 1)
        t2 = jnp.concatenate([t[:, 128:512], t[:, 0:128]], axis=1)
        gone = gone + pltpu.roll(jnp.where(lane < 16, t2, 0.0), d * 16, 1)
        t3 = jnp.concatenate([t[:, 256:512], t[:, 0:256]], axis=1)
        t3 = pltpu.roll(jnp.where((lane < 64) & (row8 == 0), t3, 0.0), (d & 7) * 64, 1)
        vec_ref[pl.ds(9 + (d >> 3), 1), :] += t3[0:1]
    vec_ref[0:8, :] = short
    vec_ref[8:9, :] = gone[0:1]
    gain, shift = vec_ref[0:1, :], vec_ref[1:2, :]
    absorb = jnp.broadcast_to(vec_ref[8:9, :], (8, WIDTH))
    ab = ab_ref[...].astype(F32).astype(BF16)

    def clear(u, _):
        here = rows_at(u * UNIT, UNIT)
        n1_ref[here, :] = jnp.zeros((UNIT, WIDTH), BF16)
        start_ref[here, :] = jnp.zeros((UNIT, WIDTH), F32)
        mix_ref[here, :] = jnp.zeros((UNIT, WIDTH), BF16)
        return 0

    lax.fori_loop(total, tiles * (TILE // UNIT), clear, 0)

    def begin(s, _):
        pltpu.make_async_copy(x_hbm.at[s], x_ref.at[s], sem_x.at[s]).wait()
        row = time_ref[pl.ds(step_ref[s], 1), :]
        mine = jnp.where(row8 == s, absorb, 0.0).astype(BF16)
        v = x_ref[s].astype(F32) + row + dot_tn(ab, mine)
        out_ref[s] = v.astype(BF16)
        pltpu.make_async_copy(out_ref.at[s], out_hbm.at[s], sem_o.at[s]).start()

        def put(n):
            here = rows_at(base_ref[s] * UNIT, n * UNIT)
            w = v[0 : n * UNIT]
            start_ref[here, :] = w
            u, _r = norm_stats(w)
            n1_ref[here, :] = (u * gain + shift).astype(BF16)

        by_class(cnt_ref[s], put)
        return 0

    lax.fori_loop(0, slots, begin, 0)
    start_tiles(tiles, (start_ref, start_hbm, sem_s), (n1_ref, n1_hbm, sem_n))

    def project(t, _):
        here = tile_at(t)
        n1 = n1_ref[here, :]
        for c in range(3):
            cols = slice(c * WIDTH, (c + 1) * WIDTH)
            p = dot_nn(n1, w_ref[:, cols])
            if c != 1:
                p = p + vec_ref[2 + c // 2 : 3 + c // 2, :]
            qkv_ref[here, cols] = p.astype(BF16)
        copies(qkv_ref, qkv_hbm, sem_q, t).start()
        return 0

    lax.fori_loop(0, tiles, project, 0)

    @pl.when((total % 4 == 0) & (total < 32))
    def _():
        qkv_ref[rows_at(total * UNIT, UNIT), :] = jnp.zeros((UNIT, 3 * WIDTH), BF16)

    def slot(s, _):
        def run(n):
            attn_fwd_slot(
                n, len_ref[s], s, base_ref[s] * UNIT, qkv_ref, mix_ref, lse_ref, ot_ref
            )

        by_class(cnt_ref[s], run)
        return 0

    lax.fori_loop(0, slots, slot, 0)
    start_tiles(tiles, (mix_ref, mix_hbm, sem_m))
    wait_tiles(
        tiles,
        (start_ref, start_hbm, sem_s),
        (n1_ref, n1_hbm, sem_n),
        (qkv_ref, qkv_hbm, sem_q),
        (mix_ref, mix_hbm, sem_m),
    )
    for s in range(slots):
        pltpu.make_async_copy(out_ref.at[s], out_hbm.at[s], sem_o.at[s]).wait()


def load_mlp(me, blocks, wu_ref, wd_ref, wp_ref):
    for q in range(32):
        d = device_of(jnp.int32(q), me)
        src = blocks[q >> 2]
        for c in range(4):
            wu_ref[rows_at(d * 16, 16, 16), c * WIDTH : (c + 1) * WIDTH] = src[
                q & 3, c * 16 : (c + 1) * 16, :
            ]
        wd_ref[rows_at(d * 64, 64, 64), :] = src[q & 3, 64:128, :]
        wp_ref[rows_at(d * 16, 16, 16), :] = src[q & 3, 128:144, :]


def gelu_pair(x):
    c0 = 0.7978845608028654
    x2 = x * x
    t = jnp.tanh(x * (c0 + (c0 * 0.044715) * x2))
    half = 0.5 + 0.5 * t
    slope = half + (0.5 * x) * (1.0 - t * t) * (c0 + (3.0 * 0.044715 * c0) * x2)
    return x * half, slope


def mlp_body(
    me_ref, len_ref, val_ref, vec_ref, mix_hbm, start_hbm, cp_hbm, out0_hbm,
    b0, b1, b2, b3, b4, b5, b6, b7,
    out_hbm, gmid_hbm, gmix_hbm, keep_ref, send_ref, vg_ref,
    mix_ref, mid_ref, cp_ref, out_ref, gmix_ref, gatt_ref, n2_ref, act_ref, gh_ref,
    wu_ref, wd_ref, wp_ref, dwu_ref, dwd_ref, gub_ref, acc_ref,
    cnt_ref, base_ref, sem_m, sem_s, sem_c, sem_g, sem_x, sem_o,
):
    slots = len_ref.shape[0]
    me = me_ref[0]
    total, tiles = slot_plan(len_ref, val_ref, cnt_ref, base_ref)
    pairs = (tiles + 1) // 2
    start_tiles(
        tiles, (mix_hbm, mix_ref, sem_m), (start_hbm, mid_ref, sem_s), (cp_hbm, cp_ref, sem_c)
    )
    load_mlp(me, (b0, b1, b2, b3, b4, b5, b6, b7), wu_ref, wd_ref, wp_ref)
    gain, shift = vec_ref[5:6, :], vec_ref[6:7, :]
    acc_ref[...] = jnp.zeros_like(acc_ref)
    gub_ref[...] = jnp.zeros_like(gub_ref)

    @pl.when(tiles % 2 == 1)
    def _():
        here = tile_at(tiles)
        for ref in (act_ref, gh_ref, n2_ref, gatt_ref, mix_ref, cp_ref):
            ref[here, :] = jnp.zeros((TILE, ref.shape[1]), BF16)

    def step(t, _):
        here = tile_at(t)
        copies(mix_hbm, mix_ref, sem_m, t).wait()
        copies(start_hbm, mid_ref, sem_s, t).wait()
        copies(cp_hbm, cp_ref, sem_c, t).wait()
        r = lax.broadcasted_iota(jnp.int32, (TILE, 1), 0) + t * TILE
        bad = r >= total * UNIT
        for s in range(slots):
            lo = base_ref[s] * UNIT
            bad = bad | ((r >= lo + len_ref[s]) & (r < lo + cnt_ref[s] * UNIT))
        mask = jnp.where(bad, 0.0, 1.0)
        att = dot_nn(mix_ref[here, :], wp_ref[...]) + vec_ref[4:5, :]
        mid = mid_ref[here, :] + mask * att
        mid_ref[here, :] = mid
        u, r = norm_stats(mid)
        n2_ref[here, :] = (u * gain + shift).astype(BF16)
        for c in range(4):
            cols = slice(c * FFC, (c + 1) * FFC)
            h = dot_nn(n2_ref[here, :], wu_ref[:, cols]) + vec_ref[9 + c : 10 + c, :]
            ga = dot_nt(cp_ref[here, :], wd_ref[cols, :])
            act, slope = gelu_pair(h)
            gh = ga * slope
            act_ref[here, cols] = act.astype(BF16)
            gh_ref[here, cols] = gh.astype(BF16)
            gub_ref[:, cols] += fold8(gh)
        y = dot_nn(act_ref[here, :], wd_ref[...]) + vec_ref[7:8, :]
        mid = mid_ref[here, :]
        out_ref[here, :] = (mid + mask * y).astype(BF16)
        u, r = norm_stats(mid)
        g2 = dot_nt(gh_ref[here, :], wu_ref[...])
        cot = cp_ref[here, :].astype(F32)
        gm = cot + norm_back(g2, u, r, gain)
        mid_ref[here, :] = gm
        ga = gm.astype(BF16)
        gatt_ref[here, :] = ga
        gmix_ref[here, :] = dot_nt(ga, wp_ref[...]).astype(BF16)
        copies(mid_ref, gmid_hbm, sem_g, t).start()
        copies(gmix_ref, gmix_hbm, sem_x, t).start()
        acc_ref[0] += fold8(g2 * u)
        acc_ref[1] += fold8(g2)
        acc_ref[2] += fold8(cot)
        acc_ref[3] += fold8(gm)
        return 0

    lax.fori_loop(0, tiles, step, 0)

    def unit(s, j):
        return pltpu.make_async_copy(
            out_ref.at[rows_at((base_ref[s] + j) * UNIT, UNIT)],
            out_hbm.at[s, pl.ds(j * UNIT, UNIT)],
            sem_o.at[s, j],
        )

    for s in range(slots):
        for j in range(4):
            pl.when(j < cnt_ref[s])(lambda s=s, j=j: unit(s, j).start())

    for c in range(4):
        cols = slice(c * FFC, (c + 1) * FFC)
        dwu_ref[...] = jnp.zeros_like(dwu_ref)
        dwd_ref[...] = jnp.zeros_like(dwd_ref)

        def weights(k, _, cols=cols):
            here = tile_at(k, PAIR)
            dwu_ref[...] += dot_tn(n2_ref[here, :], gh_ref[here, cols])
            dwd_ref[...] += dot_tn(act_ref[here, cols], cp_ref[here, :])
            return 0

        lax.fori_loop(0, pairs, weights, 0)
        for q in range(32):
            d = device_of(jnp.int32(q), me)
            dst = keep_ref if q < 16 else send_ref
            dst[q & 15, c * 16 : (c + 1) * 16, :] = dwu_ref[rows_at(d * 16, 16, 16), :].astype(BF16)
        for i in range(8):
            piece = dwd_ref[i * 64 : (i + 1) * 64, :].astype(BF16)
            place = place_of(jnp.int32(8 * c + i), me)
            for dst, at in ((keep_ref, place < 16), (send_ref, place >= 16)):
                pl.when(at)(
                    functools.partial(dst.__setitem__, (place & 15, slice(64, 128)), piece)
                )
    dwu_ref[...] = jnp.zeros_like(dwu_ref)

    def proj(k, _):
        here = tile_at(k, PAIR)
        dwu_ref[...] += dot_tn(mix_ref[here, :], gatt_ref[here, :])
        return 0

    lax.fori_loop(0, pairs, proj, 0)
    for q in range(32):
        d = device_of(jnp.int32(q), me)
        dst = keep_ref if q < 16 else send_ref
        dst[q & 15, 128:144, :] = dwu_ref[rows_at(d * 16, 16, 16), :].astype(BF16)

    def total_of(v):
        return jnp.sum(v, axis=0, keepdims=True)

    vg_ref[...] = jnp.zeros_like(vg_ref)
    vg_ref[4:5, :] = total_of(acc_ref[3])
    vg_ref[5:6, :] = total_of(acc_ref[0])
    vg_ref[6:7, :] = total_of(acc_ref[1])
    vg_ref[7:8, :] = total_of(acc_ref[2])
    for c in range(4):
        vg_ref[9 + c : 10 + c, :] = total_of(gub_ref[:, c * FFC : (c + 1) * FFC])
    for s in range(slots):
        for j in range(4):
            pl.when(j < cnt_ref[s])(lambda s=s, j=j: unit(s, j).wait())
    wait_tiles(tiles, (mid_ref, gmid_hbm, sem_g), (gmix_ref, gmix_hbm, sem_x))


def attn_bwd_slot(n, live, s, row0, qkv_ref, lse_ref, gmix_ref, gpi_ref, ot_ref):
    keep = n * UNIT
    span = max(keep, 128)
    rows = rows_at(row0, span)
    out_rows = rows_at(row0, keep)
    k_t = qkv_ref[rows, WIDTH : 2 * WIDTH].T
    lane = lax.broadcasted_iota(jnp.int32, (span, 128), 1)
    key_row = lax.broadcasted_iota(jnp.int32, (span, span), 0)
    query_col = lax.broadcasted_iota(jnp.int32, (span, span), 1)
    for hp in range(HEADS // 2):
        q2 = qkv_ref[rows, hp * 128 : (hp + 1) * 128] * BF16(0.125)
        k2 = qkv_ref[rows, WIDTH + hp * 128 : WIDTH + (hp + 1) * 128]
        v2 = qkv_ref[rows, 2 * WIDTH + hp * 128 : 2 * WIDTH + (hp + 1) * 128]
        o2 = gmix_ref[rows, hp * 128 : (hp + 1) * 128]
        gk, gv = None, None
        for half in range(2):
            h = hp * 2 + half
            here = (lane >= 64) == (half == 1)
            qm = jnp.where(here, q2, BF16(0))
            om = jnp.where(here, o2, BF16(0))
            sc = dot_nt(k2, qm)
            p = jnp.exp(sc - lse_ref[s, h : h + 1, 0:span])
            if n != 2:
                ok = key_row < live
                if n == 1:
                    ok = ok & (query_col < live)
                p = jnp.where(ok, p, 0.0)
            dp = dot_nt(v2, om)
            row = jnp.sum(p * dp, axis=0, keepdims=True)
            ds = (p * (dp - row)).astype(BF16)
            ot_ref[h * 64 : (h + 1) * 64, 0:span] = (
                dot_nn(k_t[h * 64 : (h + 1) * 64, :], ds) * 0.125
            ).astype(BF16)
            a = dot_nn(ds, qm)
            b = dot_nn(p.astype(BF16), om)
            gk = a if gk is None else gk + a
            gv = b if gv is None else gv + b
        gpi_ref[out_rows, WIDTH + hp * 128 : WIDTH + (hp + 1) * 128] = gk[0:keep].astype(BF16)
        gpi_ref[out_rows, 2 * WIDTH + hp * 128 : 2 * WIDTH + (hp + 1) * 128] = gv[0:keep].astype(
            BF16
        )
    gpi_ref[out_rows, 0:WIDTH] = ot_ref[:, 0:span].T[0:keep]


def back_body(
    me_ref, len_ref, val_ref, step_ref, lse_ref, ab_ref, vec_ref, vgin_ref, ssum_ref, asum_ref,
    qkv_hbm, gmix_hbm, n1_hbm, start_hbm, gmid_hbm, cot_hbm, ig0_hbm, b0, b1, b2, b3, b4, b5, b6, b7,
    ig_hbm, keep_ref, send_ref,
    qkv_ref, gmix_ref, n1_ref, start_ref, gmid_ref, cot_ref, ig_ref,
    w_ref, gpi_ref, dw_ref, vg_ref, tg_ref, slot_ref, ot_ref, acc_ref,
    cnt_ref, base_ref, sem_q, sem_x, sem_n, sem_s, sem_g, sem_c, sem_o,
):
    slots = len_ref.shape[0]
    me = me_ref[0]
    total, tiles = slot_plan(len_ref, val_ref, cnt_ref, base_ref)
    pairs = (tiles + 1) // 2
    start_tiles(tiles, (qkv_hbm, qkv_ref, sem_q), (gmix_hbm, gmix_ref, sem_x))
    last = cot_hbm.shape[1] - UNIT
    tail = pltpu.make_async_copy(cot_hbm.at[:, pl.ds(last, UNIT)], cot_ref, sem_c)
    tail.start()
    start_tiles(
        tiles, (n1_hbm, n1_ref, sem_n), (start_hbm, start_ref, sem_s), (gmid_hbm, gmid_ref, sem_g)
    )
    load_qkv(me, (b0, b1, b2, b3, b4, b5, b6, b7), w_ref)

    def clear(u, _):
        gpi_ref[rows_at(u * UNIT, UNIT), :] = jnp.zeros((UNIT, 3 * WIDTH), BF16)
        return 0

    lax.fori_loop(total, pairs * (PAIR // UNIT), clear, 0)

    @pl.when(tiles % 2 == 1)
    def _():
        n1_ref[tile_at(tiles), :] = jnp.zeros((TILE, WIDTH), BF16)

    wait_tiles(tiles, (qkv_hbm, qkv_ref, sem_q), (gmix_hbm, gmix_ref, sem_x))

    @pl.when((total % 4 == 0) & (total < 32))
    def _():
        here = rows_at(total * UNIT, UNIT)
        qkv_ref[here, :] = jnp.zeros((UNIT, 3 * WIDTH), BF16)
        gmix_ref[here, :] = jnp.zeros((UNIT, WIDTH), BF16)

    def slot(s, _):
        def run(n):
            attn_bwd_slot(
                n, len_ref[s], s, base_ref[s] * UNIT, qkv_ref, lse_ref, gmix_ref, gpi_ref, ot_ref
            )

        by_class(cnt_ref[s], run)
        return 0

    lax.fori_loop(0, slots, slot, 0)
    wait_tiles(tiles, (n1_hbm, n1_ref, sem_n))

    gain = vec_ref[0:1, :]
    acc_ref[...] = jnp.zeros_like(acc_ref)
    dw_ref[...] = jnp.zeros_like(dw_ref)

    def weights(k, _):
        here = tile_at(k, PAIR)
        for c in range(3):
            cols = slice(c * WIDTH, (c + 1) * WIDTH)
            g = gpi_ref[here, cols]
            dw_ref[:, cols] += dot_tn(n1_ref[here, :], g)
            if c != 1:
                acc_ref[2 + c // 2] += fold8(g.astype(F32))
        return 0

    lax.fori_loop(0, pairs, weights, 0)

    def norm(t, _):
        here = tile_at(t)
        copies(start_hbm, start_ref, sem_s, t).wait()
        copies(gmid_hbm, gmid_ref, sem_g, t).wait()
        g1 = dot_nt(gpi_ref[here, :], w_ref[...])
        u, r = norm_stats(start_ref[here, :])
        gs = gmid_ref[here, :] + norm_back(g1, u, r, gain)
        gmid_ref[here, :] = gs
        ig_ref[here, :] = gs.astype(BF16)
        acc_ref[0] += fold8(g1 * u)
        acc_ref[1] += fold8(g1)
        return 0

    lax.fori_loop(0, tiles, norm, 0)
    tail.wait()

    ab = ab_ref[...].astype(F32)
    row8 = lax.broadcasted_iota(jnp.int32, ab.shape, 0)
    tg_ref[...] = jnp.zeros_like(tg_ref)
    acc_ref[4] = asum_ref[...]
    slot_ref[...] = ssum_ref[...]

    def unit(s, j):
        return pltpu.make_async_copy(
            ig_ref.at[rows_at((base_ref[s] + j) * UNIT, UNIT)],
            ig_hbm.at[s, pl.ds(j * UNIT, UNIT)],
            sem_o.at[s, j],
        )

    upos = lax.broadcasted_iota(jnp.int32, (UNIT, 1), 0)

    def finish(s, _):
        def run(n):
            here = rows_at(base_ref[s] * UNIT, n * UNIT)
            gs = gmid_ref[here, :]
            slot_ref[pl.ds(s, 1), :] += jnp.sum(gs, axis=0, keepdims=True)
            mine = jnp.where(row8 == s, ab, 0.0).astype(BF16)[:, 0 : n * UNIT]
            acc_ref[4] += dot_nn(mine, ig_ref[here, :])
            if n == 4:
                end = rows_at((base_ref[s] + 3) * UNIT, UNIT)
                raw = cot_ref[s].astype(F32)
                ig_ref[end, :] = jnp.where(
                    upos + last < len_ref[s], ig_ref[end, :].astype(F32), raw
                ).astype(BF16)
            for j in range(n):
                unit(s, j).start()

        by_class(cnt_ref[s], run)
        tg_ref[pl.ds(step_ref[s], 1), :] += slot_ref[pl.ds(s, 1), :]
        return 0

    lax.fori_loop(0, slots, finish, 0)

    vg_ref[...] = vgin_ref[...]
    for v, a in ((0, 0), (1, 1), (2, 2), (3, 3), (8, 4)):
        vg_ref[v : v + 1, :] = jnp.sum(acc_ref[a], axis=0, keepdims=True)
    lane = lax.broadcasted_iota(jnp.int32, (8, WIDTH), 1)
    zero = jnp.zeros((8, WIDTH), F32)
    short = vg_ref[0:8, :]
    gone = jnp.broadcast_to(vg_ref[8:9, :], (8, WIDTH))
    first_row = lax.broadcasted_iota(jnp.int32, (8, WIDTH), 0) == 0
    for q in range(32):
        d = device_of(jnp.int32(q), me)
        dst = keep_ref if q < 16 else send_ref
        for c in range(3):
            dst[q & 15, c * 16 : (c + 1) * 16, :] = dw_ref[
                rows_at(d * 16, 16, 16), c * WIDTH : (c + 1) * WIDTH
            ].astype(BF16)
        back = (WIDTH - d * 16) & (WIDTH - 1)
        a = jnp.where(lane < 16, pltpu.roll(short, back, 1), zero)
        b = jnp.where((lane < 16) & first_row, pltpu.roll(gone, back, 1), zero)
        wide = jnp.broadcast_to(vg_ref[pl.ds(9 + (d >> 3), 1), :], (8, WIDTH))
        wide = pltpu.roll(wide, (WIDTH - (d & 7) * 64) & (WIDTH - 1), 1)
        w = jnp.where((lane < 64) & first_row, wide, zero)
        a = a + jnp.concatenate([zero[:, 0:128], b[:, 0:128], w[:, 0:128], zero[:, 0:128]], axis=1)
        t = tg_ref[rows_at(d * 8, 8, 8), :]
        dst[q & 15, 48:64, :] = jnp.concatenate([t, a], axis=0).astype(BF16)
    for s in range(slots):
        for j in range(4):
            pl.when(j < cnt_ref[s])(lambda s=s, j=j: unit(s, j).wait())


def pair_body(keep, got, *outs):
    for k, o in enumerate(outs):
        part = slice(4 * k, 4 * k + 4)
        o[...] = (keep[part].astype(F32) + got[part].astype(F32)).astype(BF16)


def plane_body(a, b, c, d, *outs):
    for k, o in enumerate(outs):
        o[...] = (
            (a[k].astype(F32) + b[k].astype(F32)) + (c[k].astype(F32) + d[k].astype(F32))
        ).astype(BF16)


def line_sum(a, b, c, d, lo, hi):
    at = slice(lo, hi)
    return (a[at].astype(F32) + b[at].astype(F32)) + (c[at].astype(F32) + d[at].astype(F32))


def end_mlp_body(a, b, c, d, up, down, proj):
    for k in range(4):
        up[:, k * WIDTH : (k + 1) * WIDTH] = line_sum(a, b, c, d, 16 * k, 16 * k + 16)
    down[...] = line_sum(a, b, c, d, 64, 128)
    proj[...] = line_sum(a, b, c, d, 128, 144)


def end_qkv_body(a, b, c, d, qkv, time, vec):
    for k in range(3):
        qkv[:, k * WIDTH : (k + 1) * WIDTH] = line_sum(a, b, c, d, 16 * k, 16 * k + 16)
    tail = line_sum(a, b, c, d, 48, 64)
    time[...] = tail[0:8]
    vec[...] = tail[8:16]


SMEM = pl.BlockSpec(memory_space=pltpu.SMEM)
VMEM = pl.BlockSpec(memory_space=pltpu.VMEM)
ANY = pl.BlockSpec(memory_space=pl.ANY)


def call(body, ins, outs, scratch, args, alias=None, name=None):
    return pl.pallas_call(
        body,
        out_shape=[jax.ShapeDtypeStruct(s, d) for s, d, _ in outs],
        in_specs=list(ins),
        out_specs=[m for _, _, m in outs],
        scratch_shapes=scratch,
        input_output_aliases=alias or {},
        compiler_params=pltpu.CompilerParams(vmem_limit_bytes=VMEM_BYTES),
        name=name,
    )(*args)


def dma(*shape):
    return pltpu.SemaphoreType.DMA(shape)


def vm(*shape, dtype=BF16):
    return pltpu.VMEM(shape, dtype)


def ints(n):
    return pltpu.SMEM((n,), jnp.int32)


def pack_rows(lengths, validity, cotangent, absorbed):
    slots, length, width = cotangent.shape
    return call(
        pack_body,
        [SMEM] * 2 + [VMEM] * 2,
        [
            ((slots * length, width), BF16, VMEM),
            (cotangent.shape, BF16, VMEM),
            ((slots, width), F32, VMEM),
            ((8, width), F32, VMEM),
        ],
        [ints(slots), ints(slots)],
        (lengths, validity, cotangent, absorbed),
        name="pack_rows",
    )


def front(me, lengths, validity, timesteps, inputs, absorbed, blocks, t_rows):
    slots, length, width = inputs.shape
    rows = slots * length
    return call(
        front_body,
        [SMEM] * 4 + [VMEM, ANY] + [VMEM] * 8,
        [
            ((rows, width), F32, ANY),
            ((rows, width), BF16, ANY),
            ((rows, 3 * width), BF16, ANY),
            ((rows, width), BF16, ANY),
            ((slots, HEADS, length), F32, VMEM),
            ((slots, length, width), BF16, ANY),
            ((16, width), F32, VMEM),
        ],
        [
            vm(slots, length, width),
            vm(rows, width, dtype=F32),
            vm(rows, width),
            vm(rows, 3 * width),
            vm(rows, width),
            vm(slots, length, width),
            vm(width, 3 * width),
            vm(t_rows, width, dtype=F32),
            vm(width, length),
            ints(slots),
            ints(slots),
            dma(slots),
            dma(8),
            dma(8),
            dma(8),
            dma(8),
            dma(slots),
        ],
        (me, lengths, validity, timesteps, absorbed, inputs, *blocks),
        name="front",
    )


def mlp(me, lengths, validity, mix, start, cp, vec, out0, blocks):
    slots, length, width = out0.shape
    rows = slots * length
    return call(
        mlp_body,
        [SMEM] * 3 + [VMEM] + [ANY] * 4 + [VMEM] * 8,
        [
            ((slots, length, width), BF16, ANY),
            ((rows, width), F32, ANY),
            ((rows, width), BF16, ANY),
            ((16, ROWS2, width), BF16, VMEM),
            ((16, ROWS2, width), BF16, VMEM),
            ((16, width), F32, VMEM),
        ],
        [
            vm(rows, width),
            vm(rows, width, dtype=F32),
            vm(rows, width),
            vm(rows, width),
            vm(rows, width),
            vm(rows, width),
            vm(rows, width),
            vm(rows, FF),
            vm(rows, FF),
            vm(width, FF),
            vm(FF, width),
            vm(width, width),
            vm(width, FFC, dtype=F32),
            vm(FFC, width, dtype=F32),
            vm(8, FF, dtype=F32),
            vm(4, 8, width, dtype=F32),
            ints(slots),
            ints(slots),
            dma(8),
            dma(8),
            dma(8),
            dma(8),
            dma(8),
            dma(slots, 4),
        ],
        (me, lengths, validity, vec, mix, start, cp, out0, *blocks),
        alias={7: 0},
        name="mlp",
    )


def back(
    me, lengths, validity, timesteps, qkv, lse, gmix, n1, start, gmid, cot, ig0, absorbed, vec, vg,
    ssum, asum, blocks, t_rows,
):
    slots, length, width = cot.shape
    rows = slots * length
    return call(
        back_body,
        [SMEM] * 4 + [VMEM] * 6 + [ANY] * 7 + [VMEM] * 8,
        [
            ((slots, length, width), BF16, ANY),
            ((16, ROWS1, width), BF16, VMEM),
            ((16, ROWS1, width), BF16, VMEM),
        ],
        [
            vm(rows, 3 * width),
            vm(rows, width),
            vm(rows, width),
            vm(rows, width, dtype=F32),
            vm(rows, width, dtype=F32),
            vm(slots, UNIT, width),
            vm(rows, width),
            vm(width, 3 * width),
            vm(rows, 3 * width),
            vm(width, 3 * width, dtype=F32),
            vm(16, width, dtype=F32),
            vm(t_rows, width, dtype=F32),
            vm(slots, width, dtype=F32),
            vm(width, length),
            vm(5, 8, width, dtype=F32),
            ints(slots),
            ints(slots),
            dma(8),
            dma(8),
            dma(8),
            dma(8),
            dma(8),
            pltpu.SemaphoreType.DMA,
            dma(slots, 4),
        ],
        (
            me, lengths, validity, timesteps, lse, absorbed, vec, vg, ssum, asum,
            qkv, gmix, n1, start, gmid, cot, ig0, *blocks,
        ),
        alias={16: 0},
        name="back",
    )


def hop(x, mask):
    return lax.ppermute(x, AXES, [(i, i ^ mask) for i in range(32)])


def join(parts, name):
    return call(
        join_body,
        [VMEM] * 4,
        [((4,) + parts[0].shape, BF16, VMEM)],
        [],
        parts,
        name=name,
    )[0]


def spread_line(x):
    return [x] + [hop(x, m) for m in (2, 4, 6)]


def spread_plane(b):
    plane = [b] + [hop(b, m) for m in (8, 16, 24)]
    return plane + [hop(p, 1) for p in plane]


def reduce_pair(keep, send, name):
    got = hop(send, 1)
    shape = (4,) + keep.shape[1:]
    return call(pair_body, [VMEM] * 2, [(shape, BF16, VMEM)] * 4, [], (keep, got), name=name)


def reduce_plane(parts, name):
    got = [parts[0]] + [hop(parts[k], 8 * k) for k in (1, 2, 3)]
    shape = parts[0].shape[1:]
    return call(plane_body, [VMEM] * 4, [(shape, BF16, VMEM)] * 4, [], got, name=name)


def reduce_line(parts):
    return [parts[0]] + [hop(parts[k], 2 * k) for k in (1, 2, 3)]


def column_blocks(w):
    return [w[:, c : c + WIDTH] for c in range(0, w.shape[1], WIDTH)]


def after(x, *others):
    return lax.optimization_barrier((x,) + others)[0]


def shards(
    n_dev,
    inputs,
    lengths,
    validity,
    absorbed,
    timesteps,
    attn_gain,
    attn_shift,
    query_key_value_weight,
    query_bias,
    value_bias,
    output_projection_weight,
    output_projection_bias,
    mlp_gain,
    mlp_shift,
    up_projection_weight,
    hidden_units_bias,
    down_projection_weight,
    down_output_bias,
    absorb_vector,
    time_table,
    cotangent,
):
    t_rows = time_table.shape[0] * n_dev
    vectors = [
        attn_gain, attn_shift, query_bias, value_bias, output_projection_bias,
        mlp_gain, mlp_shift, down_output_bias, absorb_vector, hidden_units_bias,
    ]
    weights = [
        query_key_value_weight, time_table, up_projection_weight, down_projection_weight,
        output_projection_weight,
    ]

    if n_dev == 32:
        me = lax.axis_index(AXES).astype(jnp.int32)
        one, two = call(
            block_body,
            [VMEM] * 15,
            [((ROWS1, WIDTH), BF16, VMEM), ((ROWS2, WIDTH), BF16, VMEM)],
            [vm(16, WIDTH, dtype=F32)],
            weights + [v.reshape(1, -1) for v in vectors],
            name="blocks",
        )
        line1 = spread_line(one)
        cp, ig0, ssum, asum = pack_rows(lengths, validity, cotangent, absorbed)
        line1[1], cp = lax.optimization_barrier((line1[1], cp))
        own1 = join(line1, "join1")
        line2 = spread_line(after(two, own1))
        blocks1 = spread_plane(own1)
        own2 = join([after(line2[0], blocks1[3])] + line2[1:], "join2")
        blocks2 = spread_plane(own2)
    else:
        me = jnp.int32(0)

        def whole(x):
            full = lax.all_gather(x, AXES, axis=0, tiled=True)
            return full.reshape((32, full.shape[0] // 32) + full.shape[1:])

        qkv_all, time_all, up_all, down_all, proj_all = [whole(w) for w in weights]
        vec_all = [whole(v) for v in vectors]
        tail = jnp.zeros((32, 8, WIDTH), BF16)
        for v in range(8):
            tail = tail.at[:, v, 0:16].set(vec_all[v])
        tail = tail.at[:, 0, 128:144].set(vec_all[8])
        tail = tail.at[:, 0, 256:320].set(vec_all[9])
        cut = lambda w: [w[:, :, c : c + WIDTH] for c in range(0, w.shape[2], WIDTH)]
        one = jnp.concatenate(cut(qkv_all) + [time_all, tail], axis=1)
        two = jnp.concatenate(cut(up_all) + [down_all, proj_all], axis=1)
        blocks1 = [one[i::2][4 * k : 4 * k + 4] for i in range(2) for k in range(4)]
        blocks2 = [two[i::2][4 * k : 4 * k + 4] for i in range(2) for k in range(4)]
        cp, ig0, ssum, asum = pack_rows(lengths, validity, cotangent, absorbed)
    me = me.reshape(1)
    start, n1, qkv, mix, lse, out0, vec = front(
        me, lengths, validity, timesteps, inputs, absorbed, blocks1, t_rows
    )
    output, gmid, gmix, keep2, send2, vg = mlp(
        me, lengths, validity, mix, start, cp, vec, out0, blocks2
    )
    input_grad, keep1, send1 = back(
        me, lengths, validity, timesteps, qkv, lse, gmix, n1, start, gmid, cotangent, ig0, absorbed,
        vec, vg, ssum, asum, blocks1, t_rows,
    )
    wide = query_key_value_weight.shape[1]
    ff = up_projection_weight.shape[1]
    if n_dev == 32:
        plane2 = reduce_pair(keep2, send2, "pair2")
        line2 = reduce_plane(plane2, "plane2")
        g_up, g_down, g_proj = call(
            end_mlp_body,
            [VMEM] * 4,
            [((16, ff), F32, VMEM), ((64, WIDTH), F32, VMEM), ((16, WIDTH), F32, VMEM)],
            [],
            reduce_line(line2),
            name="end2",
        )
        plane1 = reduce_pair(keep1, send1, "pair1")
        line1 = reduce_plane(plane1, "plane1")
        g_qkv, g_time, vec_rows = call(
            end_qkv_body,
            [VMEM] * 4,
            [((16, wide), F32, VMEM), ((8, WIDTH), F32, VMEM), ((8, WIDTH), F32, VMEM)],
            [],
            reduce_line(line1),
            name="end1",
        )
        small = [vec_rows[v, 0:16] for v in range(8)]
        small += [vec_rows[0, 128:144], vec_rows[0, 256:320]]
    else:
        g2 = jnp.stack([keep2, send2], 1).reshape((32,) + keep2.shape[1:]).astype(F32)
        g1 = jnp.stack([keep1, send1], 1).reshape((32,) + keep1.shape[1:]).astype(F32)

        def columns(g, n):
            g = jnp.concatenate([g[:, 16 * c : 16 * c + 16] for c in range(n)], axis=2)
            return g.reshape(-1, n * WIDTH)

        g_qkv, g_up = columns(g1, wide // WIDTH), columns(g2, ff // WIDTH)
        g_down, g_proj = g2[:, 64:128].reshape(-1, WIDTH), g2[:, 128:144].reshape(-1, WIDTH)
        g_time = g1[:, 48:56].reshape(-1, WIDTH)
        small = [g1[:, 56 + v, 0:16].reshape(-1) for v in range(8)]
        small += [g1[:, 56, 128:144].reshape(-1), g1[:, 56, 256:320].reshape(-1)]
    grads = [
        small[0], small[1], g_qkv, small[2], small[3], g_proj, small[4], small[5], small[6],
        g_up, small[9], g_down, small[7], small[8], g_time,
    ]
    if n_dev != 32:
        grads = [lax.psum_scatter(g, AXES, scatter_dimension=0, tiled=True) for g in grads]
    return (output, input_grad) + tuple(grads)


def solution(mesh):
    lead = P(AXES)
    n_dev = mesh.shape["dp"] * mesh.shape["fsdp"]
    return jax.shard_map(
        functools.partial(shards, n_dev),
        mesh=mesh,
        in_specs=(lead,) * 21,
        out_specs=(lead,) * 17,
        check_vma=False,
    )
```

```python
import functools

import jax
import jax.numpy as jnp
from jax import lax
from jax.experimental import pallas as pl
from jax.experimental.pallas import tpu as pltpu
from jax.sharding import PartitionSpec as P

HEADS = 8
EPS = 1e-05
NEG = -1e30
AXES = ("dp", "fsdp")
WIDTH = 512
FF = 2048
UNIT = 64
TILE = 256
FFC = 512
ROWS1 = 64
ROWS2 = 144
VMEM_BYTES = 60 * 1024 * 1024
F32 = jnp.float32
BF16 = jnp.bfloat16


def dot_nn(a, b):
    return lax.dot_general(a, b, (((1,), (0,)), ((), ())), preferred_element_type=F32)


def dot_nt(a, b):
    return lax.dot_general(a, b, (((1,), (1,)), ((), ())), preferred_element_type=F32)


def dot_tn(a, b):
    return lax.dot_general(a, b, (((0,), (0,)), ((), ())), preferred_element_type=F32)


def rows_at(start, size, step=UNIT):
    return pl.ds(pl.multiple_of(start, step), size)


def tile_at(t, size=TILE):
    return rows_at(t * size, size, size)


def slot_plan(len_ref, val_ref, cnt_ref, base_ref):
    total = jnp.int32(0)
    for s in range(len_ref.shape[0]):
        n = jnp.where(val_ref[s] > 0, (len_ref[s] + (UNIT - 1)) // UNIT, 0)
        cnt_ref[s] = n
        base_ref[s] = total
        total = total + n
    return total, (total * UNIT + TILE - 1) // TILE


def by_class(count, fn):
    for n in (1, 2, 4):
        pl.when(count == n)(functools.partial(fn, n))


def norm_stats(v):
    mean = jnp.mean(v, axis=-1, keepdims=True)
    c = v - mean
    r = lax.rsqrt(jnp.mean(c * c, axis=-1, keepdims=True) + EPS)
    return c * r, r


def norm_back(grad, u, r, gain):
    e = grad * gain
    return r * (
        e - jnp.mean(e, axis=-1, keepdims=True) - u * jnp.mean(e * u, axis=-1, keepdims=True)
    )


def fold8(v):
    return jnp.sum(v.reshape(v.shape[0] // 8, 8, v.shape[1]), axis=0)


def copies(src, dst, sem, t):
    return pltpu.make_async_copy(src.at[tile_at(t)], dst.at[tile_at(t)], sem.at[t])


def start_tiles(tiles, *triples):
    for t in range(8):

        @pl.when(t < tiles)
        def _(t=t):
            for src, dst, sem in triples:
                copies(src, dst, sem, t).start()


def wait_tiles(tiles, *triples):
    for t in range(8):

        @pl.when(t < tiles)
        def _(t=t):
            for src, dst, sem in triples:
                copies(src, dst, sem, t).wait()


def device_of(q, me):
    return jnp.bitwise_xor(((q & 15) << 1) | (q >> 4), me)


def place_of(d, me):
    p = jnp.bitwise_xor(d, me)
    return (p & 1) * 16 + (p >> 1)


def block_body(*refs):
    qkv, time, up, down, proj = refs[:5]
    vecs = refs[5:15]
    one_ref, two_ref, tail_ref = refs[15:]
    for c in range(3):
        one_ref[c * 16 : (c + 1) * 16, :] = qkv[:, c * WIDTH : (c + 1) * WIDTH]
    tail_ref[...] = jnp.zeros_like(tail_ref)
    tail_ref[0:8, :] = time[...].astype(F32)
    for v in range(8):
        tail_ref[8 + v : 9 + v, 0:16] = vecs[v][...].astype(F32)
    tail_ref[8:9, 128:144] = vecs[8][...].astype(F32)
    tail_ref[8:9, 256:320] = vecs[9][...].astype(F32)
    one_ref[48:64, :] = tail_ref[...].astype(BF16)
    for c in range(4):
        two_ref[c * 16 : (c + 1) * 16, :] = up[:, c * WIDTH : (c + 1) * WIDTH]
    two_ref[64:128, :] = down[...]
    two_ref[128:144, :] = proj[...]


def join_body(a, b, c, d, o):
    o[0], o[1], o[2], o[3] = a[...], b[...], c[...], d[...]


def pack_body(len_ref, val_ref, cot_ref, ab_ref, cp_ref, ig_ref, ssum_ref, asum_ref, cnt_ref, base_ref):
    slots, length, _ = cot_ref.shape
    total, tiles = slot_plan(len_ref, val_ref, cnt_ref, base_ref)

    def clear(u, _):
        cp_ref[rows_at(u * UNIT, UNIT), :] = jnp.zeros((UNIT, WIDTH), BF16)
        return 0

    lax.fori_loop(total, tiles * (TILE // UNIT), clear, 0)
    pl.when(tiles % 2 == 1)(
        lambda: cp_ref.__setitem__((tile_at(tiles), slice(None)), jnp.zeros((TILE, WIDTH), BF16))
    )
    ab_t = ab_ref[...].astype(F32).T
    asum = jnp.zeros((8, WIDTH), F32)
    pos = lax.broadcasted_iota(jnp.int32, (length, 1), 0)
    for s in range(slots):
        live = jnp.where(val_ref[s] > 0, len_ref[s], 0)
        raw = cot_ref[s]
        ig_ref[s] = raw
        v = raw.astype(F32)
        ok = pos < live

        def put(n, s=s, v=v, ok=ok):
            size = n * UNIT
            cp_ref[rows_at(base_ref[s] * UNIT, size), :] = jnp.where(ok, v, 0.0)[0:size].astype(BF16)

        by_class(cnt_ref[s], put)
        rest = jnp.where(ok, 0.0, v)
        ssum_ref[s : s + 1, :] = jnp.sum(rest, axis=0, keepdims=True)
        asum = asum + fold8(rest * ab_t[:, s : s + 1])
    asum_ref[...] = asum


def load_qkv(me, blocks, w_ref):
    for q in range(32):
        d = device_of(jnp.int32(q), me)
        for c in range(3):
            w_ref[rows_at(d * 16, 16, 16), c * WIDTH : (c + 1) * WIDTH] = blocks[q >> 2][
                q & 3, c * 16 : (c + 1) * 16, :
            ]


def pipeline(first, second, third):
    first(0)
    first(1)
    for hp in range(HEADS // 2):
        if hp < HEADS // 2 - 1:
            first(2 * hp + 2)
            first(2 * hp + 3)
        second(2 * hp)
        second(2 * hp + 1)
        third(hp)


def attn_fwd_slot(n, live, s, row0, qkv_ref, mix_ref, lse_ref, ot_ref, vt_ref, s_ref, e_ref):
    keep = n * UNIT
    span = max(keep, 128)
    rows = rows_at(row0, span)
    v_t = qkv_ref[rows, 2 * WIDTH : 3 * WIDTH].T
    for h in range(HEADS):
        vt_ref[h, 0:64, 0:span] = v_t[h * 64 : (h + 1) * 64, :]
    lane = lax.broadcasted_iota(jnp.int32, (span, 128), 1)

    def scores(h):
        hp = h // 2
        q2 = qkv_ref[rows, hp * 128 : (hp + 1) * 128] * BF16(0.125)
        qm = jnp.where((lane >= 64) == (h % 2 == 1), q2, BF16(0))
        k2 = qkv_ref[rows, WIDTH + hp * 128 : WIDTH + (hp + 1) * 128]
        s_ref[h, 0:span, 0:span] = dot_nt(k2, qm)
        if n == 1:
            s_ref[h, keep:span, 0:span] = jnp.full((span - keep, span), NEG, F32)
        if n == 4:
            tail = lax.broadcasted_iota(jnp.int32, (8, span), 0) + (span - 8)
            s_ref[h, span - 8 : span, 0:span] = jnp.where(
                tail < live, s_ref[h, span - 8 : span, 0:span], NEG
            )

    def weigh(h):
        top = jnp.max(s_ref[h, 0:span, 0:span], axis=0, keepdims=True)
        lse_ref[s, h : h + 1, 0:span] = top
        e_ref[h, 0:span, 0:span] = jnp.exp(s_ref[h, 0:span, 0:span] - top).astype(BF16)

    def products(hp):
        for h in (2 * hp, 2 * hp + 1):
            o = dot_nn(vt_ref[h, :, 0:span], e_ref[h, 0:span, 0:span])
            tot = o[64:65]
            ot_ref[h * 64 : (h + 1) * 64, 0:span] = (o[0:64] * (1.0 / tot)).astype(BF16)
            lse_ref[s, h : h + 1, 0:span] += jnp.log(tot)

    pipeline(scores, weigh, products)
    mix_ref[rows_at(row0, keep), :] = ot_ref[:, 0:span].T[0:keep]


def front_body(
    me_ref, len_ref, val_ref, step_ref, ab_ref, x_hbm, b0, b1, b2, b3, b4, b5, b6, b7,
    start_hbm, n1_hbm, qkv_hbm, mix_hbm, lse_ref, out_hbm, vec_ref,
    x_ref, start_ref, n1_ref, qkv_ref, mix_ref, out_ref, w_ref, time_ref, ot_ref, vt_ref, s_ref, e_ref,
    cnt_ref, base_ref, sem_x, sem_s, sem_n, sem_q, sem_m, sem_o,
):
    slots, length, _ = x_ref.shape
    blocks = (b0, b1, b2, b3, b4, b5, b6, b7)
    me = me_ref[0]
    for s in range(slots):
        pltpu.make_async_copy(x_hbm.at[s], x_ref.at[s], sem_x.at[s]).start()
    total, tiles = slot_plan(len_ref, val_ref, cnt_ref, base_ref)
    load_qkv(me, blocks, w_ref)
    lane = lax.broadcasted_iota(jnp.int32, (8, WIDTH), 1)
    row8 = lax.broadcasted_iota(jnp.int32, (8, WIDTH), 0)
    short = jnp.zeros((8, WIDTH), F32)
    gone = jnp.zeros((8, WIDTH), F32)
    vec_ref[...] = jnp.zeros_like(vec_ref)
    for q in range(32):
        d = device_of(jnp.int32(q), me)
        tail = blocks[q >> 2][q & 3, 48:64, :].astype(F32)
        time_ref[rows_at(d * 8, 8, 8), :] = tail[0:8]
        t = tail[8:16]
        short = short + pltpu.roll(jnp.where(lane < 16, t, 0.0), d * 16, 1)
        t2 = jnp.concatenate([t[:, 128:512], t[:, 0:128]], axis=1)
        gone = gone + pltpu.roll(jnp.where(lane < 16, t2, 0.0), d * 16, 1)
        t3 = jnp.concatenate([t[:, 256:512], t[:, 0:256]], axis=1)
        t3 = pltpu.roll(jnp.where((lane < 64) & (row8 == 0), t3, 0.0), (d & 7) * 64, 1)
        vec_ref[pl.ds(9 + (d >> 3), 1), :] += t3[0:1]
    vec_ref[0:8, :] = short
    vec_ref[8:9, :] = gone[0:1]
    gain, shift = vec_ref[0:1, :], vec_ref[1:2, :]
    absorb = jnp.broadcast_to(vec_ref[8:9, :], (8, WIDTH))
    ab = ab_ref[...].astype(F32).astype(BF16)

    def clear(u, _):
        here = rows_at(u * UNIT, UNIT)
        n1_ref[here, :] = jnp.zeros((UNIT, WIDTH), BF16)
        start_ref[here, :] = jnp.zeros((UNIT, WIDTH), F32)
        mix_ref[here, :] = jnp.zeros((UNIT, WIDTH), BF16)
        return 0

    lax.fori_loop(total, tiles * (TILE // UNIT), clear, 0)

    def begin(s, _):
        pltpu.make_async_copy(x_hbm.at[s], x_ref.at[s], sem_x.at[s]).wait()
        row = time_ref[pl.ds(step_ref[s], 1), :]
        mine = jnp.where(row8 == s, absorb, 0.0).astype(BF16)
        v = x_ref[s].astype(F32) + row + dot_tn(ab, mine)
        out_ref[s] = v.astype(BF16)
        pltpu.make_async_copy(out_ref.at[s], out_hbm.at[s], sem_o.at[s]).start()

        def put(n):
            here = rows_at(base_ref[s] * UNIT, n * UNIT)
            w = v[0 : n * UNIT]
            start_ref[here, :] = w
            u, _r = norm_stats(w)
            n1_ref[here, :] = (u * gain + shift).astype(BF16)

        by_class(cnt_ref[s], put)
        return 0

    lax.fori_loop(0, slots, begin, 0)
    start_tiles(tiles, (start_ref, start_hbm, sem_s), (n1_ref, n1_hbm, sem_n))

    def project(t, _):
        here = tile_at(t)
        n1 = n1_ref[here, :]
        for c in range(3):
            cols = slice(c * WIDTH, (c + 1) * WIDTH)
            p = dot_nn(n1, w_ref[:, cols])
            if c != 1:
                p = p + vec_ref[2 + c // 2 : 3 + c // 2, :]
            qkv_ref[here, cols] = p.astype(BF16)
        copies(qkv_ref, qkv_hbm, sem_q, t).start()
        return 0

    lax.fori_loop(0, tiles, project, 0)

    @pl.when((total % 4 == 0) & (total < 32))
    def _():
        qkv_ref[rows_at(total * UNIT, UNIT), :] = jnp.zeros((UNIT, 3 * WIDTH), BF16)

    vt_ref[:, 64:80, :] = jnp.ones((HEADS, 16, length), BF16)

    def slot(s, _):
        def run(n):
            attn_fwd_slot(
                n, len_ref[s], s, base_ref[s] * UNIT, qkv_ref, mix_ref, lse_ref, ot_ref, vt_ref, s_ref,
                e_ref,
            )

        by_class(cnt_ref[s], run)
        return 0

    lax.fori_loop(0, slots, slot, 0)
    start_tiles(tiles, (mix_ref, mix_hbm, sem_m))
    wait_tiles(
        tiles,
        (start_ref, start_hbm, sem_s),
        (n1_ref, n1_hbm, sem_n),
        (qkv_ref, qkv_hbm, sem_q),
        (mix_ref, mix_hbm, sem_m),
    )
    for s in range(slots):
        pltpu.make_async_copy(out_ref.at[s], out_hbm.at[s], sem_o.at[s]).wait()


def load_mlp(me, blocks, wu_ref, wd_ref, wp_ref):
    for q in range(32):
        d = device_of(jnp.int32(q), me)
        src = blocks[q >> 2]
        for c in range(4):
            wu_ref[rows_at(d * 16, 16, 16), c * WIDTH : (c + 1) * WIDTH] = src[
                q & 3, c * 16 : (c + 1) * 16, :
            ]
        wd_ref[rows_at(d * 64, 64, 64), :] = src[q & 3, 64:128, :]
        wp_ref[rows_at(d * 16, 16, 16), :] = src[q & 3, 128:144, :]


def gelu_pair(x):
    c0 = 0.7978845608028654
    x2 = x * x
    t = jnp.tanh(x * (c0 + (c0 * 0.044715) * x2))
    half = 0.5 + 0.5 * t
    slope = half + (0.5 * x) * (1.0 - t * t) * (c0 + (3.0 * 0.044715 * c0) * x2)
    return x * half, slope


def by_tiles(tiles, fn):
    for t in range(1, 9):
        pl.when(tiles == t)(functools.partial(fn, t * TILE))


def up_body(
    me_ref, len_ref, val_ref, vec_ref, mix_hbm, start_hbm, cp_hbm, b0, b1, b2, b3, b4, b5, b6, b7,
    mid_hbm, act_hbm, gh_hbm, keep_ref, send_ref, vg_ref,
    mix_ref, mid_ref, cp_ref, n2_ref, act_ref, gh_ref, h_ref, ga_ref,
    wu_ref, wd_ref, wp_ref, dwu_ref, dwd_ref, gub_ref, acc_ref,
    cnt_ref, base_ref, sem_m, sem_s, sem_c, sem_d, sem_a, sem_g,
):
    slots = len_ref.shape[0]
    me = me_ref[0]
    total, tiles = slot_plan(len_ref, val_ref, cnt_ref, base_ref)
    start_tiles(
        tiles, (mix_hbm, mix_ref, sem_m), (start_hbm, mid_ref, sem_s), (cp_hbm, cp_ref, sem_c)
    )
    load_mlp(me, (b0, b1, b2, b3, b4, b5, b6, b7), wu_ref, wd_ref, wp_ref)
    gain, shift = vec_ref[5:6, :], vec_ref[6:7, :]
    acc_ref[...] = jnp.zeros_like(acc_ref)
    gub_ref[...] = jnp.zeros_like(gub_ref)

    def step(t, _):
        here = tile_at(t)
        copies(mix_hbm, mix_ref, sem_m, t).wait()
        copies(start_hbm, mid_ref, sem_s, t).wait()
        copies(cp_hbm, cp_ref, sem_c, t).wait()
        mask = row_mask(t, total, len_ref, cnt_ref, base_ref)

        def matmuls(c):
            cols = slice(c * FFC, (c + 1) * FFC)
            h_ref[c & 1] = dot_nn(n2_ref[here, :], wu_ref[:, cols]) + vec_ref[9 + c : 10 + c, :]
            ga_ref[c & 1] = dot_nt(cp_ref[here, :], wd_ref[cols, :])

        def curve(c):
            cols = slice(c * FFC, (c + 1) * FFC)
            act, slope = gelu_pair(h_ref[c & 1])
            gh = ga_ref[c & 1] * slope
            act_ref[here, cols] = act.astype(BF16)
            gh_ref[here, cols] = gh.astype(BF16)
            gub_ref[:, cols] += fold8(gh)

        att = dot_nn(mix_ref[here, :], wp_ref[...]) + vec_ref[4:5, :]
        mid = mid_ref[here, :] + mask * att
        mid_ref[here, :] = mid
        copies(mid_ref, mid_hbm, sem_d, t).start()
        u, _r = norm_stats(mid)
        n2_ref[here, :] = (u * gain + shift).astype(BF16)
        matmuls(0)
        for c in range(1, 4):
            matmuls(c)
            curve(c - 1)
        curve(3)
        acc_ref[...] += fold8(cp_ref[here, :].astype(F32))
        copies(act_ref, act_hbm, sem_a, t).start()
        copies(gh_ref, gh_hbm, sem_g, t).start()
        return 0

    lax.fori_loop(0, tiles, step, 0)

    @pl.when(tiles == 0)
    def _():
        dwu_ref[...] = jnp.zeros_like(dwu_ref)
        dwd_ref[...] = jnp.zeros_like(dwd_ref)

    def weights(c, _):
        cols = pl.ds(pl.multiple_of(c * FFC, FFC), FFC)

        def run(k):
            dwu_ref[...] = dot_tn(n2_ref[0:k, :], gh_ref[0:k, cols])
            dwd_ref[...] = dot_tn(act_ref[0:k, cols], cp_ref[0:k, :])

        by_tiles(tiles, run)
        for q in range(32):
            d = device_of(jnp.int32(q), me)
            dst = keep_ref if q < 16 else send_ref
            dst[q & 15, rows_at(c * 16, 16, 16), :] = dwu_ref[rows_at(d * 16, 16, 16), :].astype(
                BF16
            )
        for i in range(8):
            piece = dwd_ref[i * 64 : (i + 1) * 64, :].astype(BF16)
            place = place_of(8 * c + i, me)
            for dst, at in ((keep_ref, place < 16), (send_ref, place >= 16)):
                pl.when(at)(
                    functools.partial(dst.__setitem__, (place & 15, slice(64, 128)), piece)
                )
        return 0

    lax.fori_loop(0, 4, weights, 0)
    vg_ref[...] = jnp.zeros_like(vg_ref)
    vg_ref[7:8, :] = total_of(acc_ref[...])
    for c in range(4):
        vg_ref[9 + c : 10 + c, :] = total_of(gub_ref[:, c * FFC : (c + 1) * FFC])
    wait_tiles(
        tiles, (mid_ref, mid_hbm, sem_d), (act_ref, act_hbm, sem_a), (gh_ref, gh_hbm, sem_g)
    )


def row_mask(t, total, len_ref, cnt_ref, base_ref):
    r = lax.broadcasted_iota(jnp.int32, (TILE, 1), 0) + t * TILE
    bad = r >= total * UNIT
    for s in range(len_ref.shape[0]):
        lo = base_ref[s] * UNIT
        bad = bad | ((r >= lo + len_ref[s]) & (r < lo + cnt_ref[s] * UNIT))
    return jnp.where(bad, 0.0, 1.0)


def total_of(v):
    return jnp.sum(v, axis=0, keepdims=True)


def down_body(
    me_ref, len_ref, val_ref, vec_ref, vgin_ref, mix_hbm, mid_hbm, cp_hbm, act_hbm, gh_hbm, out0_hbm,
    b0, b1, b2, b3, b4, b5, b6, b7,
    out_hbm, gmid_hbm, gmix_hbm, dwp_ref, vg_ref,
    mix_ref, mid_ref, cp_ref, act_ref, gh_ref, out_ref, gmix_ref, gatt_ref,
    wu_ref, wd_ref, wp_ref, acc_ref,
    cnt_ref, base_ref, sem_m, sem_s, sem_c, sem_a, sem_h, sem_g, sem_x, sem_o,
):
    slots = len_ref.shape[0]
    me = me_ref[0]
    total, tiles = slot_plan(len_ref, val_ref, cnt_ref, base_ref)
    start_tiles(
        tiles,
        (act_hbm, act_ref, sem_a),
        (gh_hbm, gh_ref, sem_h),
        (mid_hbm, mid_ref, sem_s),
        (cp_hbm, cp_ref, sem_c),
        (mix_hbm, mix_ref, sem_m),
    )
    load_mlp(me, (b0, b1, b2, b3, b4, b5, b6, b7), wu_ref, wd_ref, wp_ref)
    gain = vec_ref[5:6, :]
    acc_ref[...] = jnp.zeros_like(acc_ref)

    def step(t, _):
        here = tile_at(t)
        copies(act_hbm, act_ref, sem_a, t).wait()
        copies(gh_hbm, gh_ref, sem_h, t).wait()
        copies(mid_hbm, mid_ref, sem_s, t).wait()
        copies(cp_hbm, cp_ref, sem_c, t).wait()
        mask = row_mask(t, total, len_ref, cnt_ref, base_ref)
        g2 = dot_nt(gh_ref[here, :], wu_ref[...])
        y = dot_nn(act_ref[here, :], wd_ref[...]) + vec_ref[7:8, :]
        mid = mid_ref[here, :]
        out_ref[here, :] = (mid + mask * y).astype(BF16)
        u, r = norm_stats(mid)
        gm = cp_ref[here, :].astype(F32) + norm_back(g2, u, r, gain)
        mid_ref[here, :] = gm
        ga = gm.astype(BF16)
        gatt_ref[here, :] = ga
        gmix_ref[here, :] = dot_nt(ga, wp_ref[...]).astype(BF16)
        copies(mid_ref, gmid_hbm, sem_g, t).start()
        copies(gmix_ref, gmix_hbm, sem_x, t).start()
        acc_ref[0] += fold8(g2 * u)
        acc_ref[1] += fold8(g2)
        acc_ref[2] += fold8(gm)
        return 0

    lax.fori_loop(0, tiles, step, 0)

    def unit(s, j):
        return pltpu.make_async_copy(
            out_ref.at[rows_at((base_ref[s] + j) * UNIT, UNIT)],
            out_hbm.at[s, pl.ds(j * UNIT, UNIT)],
            sem_o.at[s, j],
        )

    for s in range(slots):
        for j in range(4):
            pl.when(j < cnt_ref[s])(lambda s=s, j=j: unit(s, j).start())
    wait_tiles(tiles, (mix_hbm, mix_ref, sem_m))
    pl.when(tiles == 0)(lambda: dwp_ref.__setitem__(..., jnp.zeros_like(dwp_ref)))

    def proj(k):
        dwp_ref[...] = dot_tn(mix_ref[0:k, :], gatt_ref[0:k, :]).astype(BF16)

    by_tiles(tiles, proj)
    vg_ref[...] = vgin_ref[...]
    vg_ref[4:5, :] = total_of(acc_ref[2])
    vg_ref[5:6, :] = total_of(acc_ref[0])
    vg_ref[6:7, :] = total_of(acc_ref[1])
    for s in range(slots):
        for j in range(4):
            pl.when(j < cnt_ref[s])(lambda s=s, j=j: unit(s, j).wait())
    wait_tiles(tiles, (mid_ref, gmid_hbm, sem_g), (gmix_ref, gmix_hbm, sem_x))


def attn_bwd_slot(
    n, live, s, row0, qkv_ref, lse_ref, gmix_ref, gpi_ref, ot_ref, s_ref, dp_ref, p_ref, ds_ref
):
    keep = n * UNIT
    span = max(keep, 128)
    rows = rows_at(row0, span)
    out_rows = rows_at(row0, keep)
    k_t = qkv_ref[rows, WIDTH : 2 * WIDTH].T
    lane = lax.broadcasted_iota(jnp.int32, (span, 128), 1)
    key_row = lax.broadcasted_iota(jnp.int32, (span, span), 0)
    query_col = lax.broadcasted_iota(jnp.int32, (span, span), 1)

    def halves(ref, base, h, scale=None):
        hp = h // 2
        v = ref[rows, base + hp * 128 : base + (hp + 1) * 128]
        if scale is not None:
            v = v * BF16(scale)
        return jnp.where((lane >= 64) == (h % 2 == 1), v, BF16(0))

    def whole(base, h):
        return qkv_ref[rows, base + (h // 2) * 128 : base + (h // 2 + 1) * 128]

    def scores(h):
        s_ref[h, 0:span, 0:span] = dot_nt(whole(WIDTH, h), halves(qkv_ref, 0, h, 0.125))
        dp_ref[h, 0:span, 0:span] = dot_nt(whole(2 * WIDTH, h), halves(gmix_ref, 0, h))

    def weigh(h):
        p = jnp.exp(s_ref[h, 0:span, 0:span] - lse_ref[s, h : h + 1, 0:span])
        if n != 2:
            ok = key_row < live
            if n == 1:
                ok = ok & (query_col < live)
            p = jnp.where(ok, p, 0.0)
        p_ref[h, 0:span, 0:span] = p.astype(BF16)
        row = jnp.sum(p * dp_ref[h, 0:span, 0:span], axis=0, keepdims=True)
        ds_ref[h, 0:span, 0:span] = (p * (dp_ref[h, 0:span, 0:span] - row)).astype(BF16)

    def products(hp):
        gk, gv = None, None
        for h in (2 * hp, 2 * hp + 1):
            ds = ds_ref[h, 0:span, 0:span]
            ot_ref[h * 64 : (h + 1) * 64, 0:span] = (
                dot_nn(k_t[h * 64 : (h + 1) * 64, :], ds) * 0.125
            ).astype(BF16)
            a = dot_nn(ds, halves(qkv_ref, 0, h, 0.125))
            b = dot_nn(p_ref[h, 0:span, 0:span], halves(gmix_ref, 0, h))
            gk = a if gk is None else gk + a
            gv = b if gv is None else gv + b
        lo, hi = hp * 128, (hp + 1) * 128
        gpi_ref[out_rows, WIDTH + lo : WIDTH + hi] = gk[0:keep].astype(BF16)
        gpi_ref[out_rows, 2 * WIDTH + lo : 2 * WIDTH + hi] = gv[0:keep].astype(BF16)

    pipeline(scores, weigh, products)
    gpi_ref[out_rows, 0:WIDTH] = ot_ref[:, 0:span].T[0:keep]


def attn_body(
    len_ref, val_ref, lse_ref, qkv_hbm, gmix_hbm, gpi_hbm,
    qkv_ref, gmix_ref, gpi_ref, ot_ref, s_ref, dp_ref, p_ref, ds_ref,
    cnt_ref, base_ref, sem_q, sem_x, sem_o,
):
    slots = len_ref.shape[0]
    total, tiles = slot_plan(len_ref, val_ref, cnt_ref, base_ref)
    loads = ((qkv_hbm, qkv_ref, sem_q), (gmix_hbm, gmix_ref, sem_x))
    start_tiles(tiles, *loads)
    wait_tiles(tiles, *loads)

    @pl.when((total % 4 == 0) & (total < 32))
    def _():
        here = rows_at(total * UNIT, UNIT)
        for ref in (qkv_ref, gmix_ref):
            ref[here, :] = jnp.zeros((UNIT, ref.shape[1]), BF16)

    def done(s, n):
        here = rows_at(base_ref[s] * UNIT, n * UNIT)
        return pltpu.make_async_copy(gpi_ref.at[here], gpi_hbm.at[here], sem_o.at[s])

    def slot(s, _):
        def run(n):
            attn_bwd_slot(
                n, len_ref[s], s, base_ref[s] * UNIT, qkv_ref, lse_ref, gmix_ref, gpi_ref,
                ot_ref, s_ref, dp_ref, p_ref, ds_ref,
            )
            done(s, n).start()

        by_class(cnt_ref[s], run)
        return 0

    lax.fori_loop(0, slots, slot, 0)
    for s in range(slots):
        by_class(cnt_ref[s], lambda n, s=s: done(s, n).wait())


def weights_body(
    me_ref, len_ref, val_ref, dwp_ref, vgin_ref, gpi_hbm, n1_hbm, keep_ref, send_ref, vg_ref,
    gpi_ref, n1_ref, dw_ref, acc_ref, cnt_ref, base_ref, sem_q, sem_n,
):
    me = me_ref[0]
    total, tiles = slot_plan(len_ref, val_ref, cnt_ref, base_ref)
    loads = ((gpi_hbm, gpi_ref, sem_q), (n1_hbm, n1_ref, sem_n))
    start_tiles(tiles, *loads)
    for q in range(32):
        d = device_of(jnp.int32(q), me)
        dst = keep_ref if q < 16 else send_ref
        dst[q & 15, 48:64, :] = dwp_ref[rows_at(d * 16, 16, 16), :]
    acc_ref[...] = jnp.zeros_like(acc_ref)
    wait_tiles(tiles, *loads)

    def clear(u, _):
        gpi_ref[rows_at(u * UNIT, UNIT), :] = jnp.zeros((UNIT, 3 * WIDTH), BF16)
        return 0

    lax.fori_loop(total, tiles * (TILE // UNIT), clear, 0)
    pl.when(tiles == 0)(lambda: dw_ref.__setitem__(..., jnp.zeros_like(dw_ref)))

    def column(c, _):
        cols = pl.ds(pl.multiple_of(c * WIDTH, WIDTH), WIDTH)

        def run(k):
            dw_ref[...] = dot_tn(n1_ref[0:k, :], gpi_ref[0:k, cols])
            acc_ref[c] = fold8(gpi_ref[0:k, cols].astype(F32))

        by_tiles(tiles, run)
        for q in range(32):
            d = device_of(jnp.int32(q), me)
            dst = keep_ref if q < 16 else send_ref
            dst[q & 15, rows_at(c * 16, 16, 16), :] = dw_ref[rows_at(d * 16, 16, 16), :].astype(
                BF16
            )
        return 0

    lax.fori_loop(0, 3, column, 0)
    vg_ref[...] = vgin_ref[...]
    vg_ref[2:3, :] = total_of(acc_ref[0])
    vg_ref[3:4, :] = total_of(acc_ref[2])


def back_body(
    me_ref, len_ref, val_ref, step_ref, ab_ref, vec_ref, vgin_ref, ssum_ref, asum_ref,
    gpi_hbm, start_hbm, gmid_hbm, cot_hbm, ig0_hbm, b0, b1, b2, b3, b4, b5, b6, b7,
    ig_hbm, keep_ref, send_ref,
    gpi_ref, start_ref, gmid_ref, cot_ref, ig_ref,
    w_ref, vg_ref, tg_ref, slot_ref, acc_ref,
    cnt_ref, base_ref, sem_q, sem_s, sem_g, sem_c, sem_o,
):
    slots = len_ref.shape[0]
    me = me_ref[0]
    total, tiles = slot_plan(len_ref, val_ref, cnt_ref, base_ref)
    start_tiles(
        tiles,
        (gpi_hbm, gpi_ref, sem_q),
        (start_hbm, start_ref, sem_s),
        (gmid_hbm, gmid_ref, sem_g),
    )
    last = cot_hbm.shape[1] - UNIT
    tail = pltpu.make_async_copy(cot_hbm.at[:, pl.ds(last, UNIT)], cot_ref, sem_c)
    tail.start()
    load_qkv(me, (b0, b1, b2, b3, b4, b5, b6, b7), w_ref)
    gain = vec_ref[0:1, :]
    acc_ref[...] = jnp.zeros_like(acc_ref)

    def norm(t, _):
        here = tile_at(t)
        copies(gpi_hbm, gpi_ref, sem_q, t).wait()
        copies(start_hbm, start_ref, sem_s, t).wait()
        copies(gmid_hbm, gmid_ref, sem_g, t).wait()

        @pl.when(t == tiles - 1)
        def _():
            def clear(u, _):
                gpi_ref[rows_at(u * UNIT, UNIT), :] = jnp.zeros((UNIT, 3 * WIDTH), BF16)
                return 0

            lax.fori_loop(total, tiles * (TILE // UNIT), clear, 0)

        g1 = dot_nt(gpi_ref[here, :], w_ref[...])
        u, r = norm_stats(start_ref[here, :])
        gs = gmid_ref[here, :] + norm_back(g1, u, r, gain)
        gmid_ref[here, :] = gs
        ig_ref[here, :] = gs.astype(BF16)
        acc_ref[0] += fold8(g1 * u)
        acc_ref[1] += fold8(g1)
        return 0

    lax.fori_loop(0, tiles, norm, 0)
    tail.wait()

    ab = ab_ref[...].astype(F32)
    row8 = lax.broadcasted_iota(jnp.int32, ab.shape, 0)
    tg_ref[...] = jnp.zeros_like(tg_ref)
    acc_ref[2] = asum_ref[...]
    slot_ref[...] = ssum_ref[...]

    def unit(s, j):
        return pltpu.make_async_copy(
            ig_ref.at[rows_at((base_ref[s] + j) * UNIT, UNIT)],
            ig_hbm.at[s, pl.ds(j * UNIT, UNIT)],
            sem_o.at[s, j],
        )

    upos = lax.broadcasted_iota(jnp.int32, (UNIT, 1), 0)

    def finish(s, _):
        def run(n):
            here = rows_at(base_ref[s] * UNIT, n * UNIT)
            gs = gmid_ref[here, :]
            slot_ref[pl.ds(s, 1), :] += jnp.sum(gs, axis=0, keepdims=True)
            mine = jnp.where(row8 == s, ab, 0.0).astype(BF16)[:, 0 : n * UNIT]
            acc_ref[2] += dot_nn(mine, ig_ref[here, :])
            if n == 4:
                end = rows_at((base_ref[s] + 3) * UNIT, UNIT)
                raw = cot_ref[s].astype(F32)
                ig_ref[end, :] = jnp.where(
                    upos + last < len_ref[s], ig_ref[end, :].astype(F32), raw
                ).astype(BF16)
            for j in range(n):
                unit(s, j).start()

        by_class(cnt_ref[s], run)
        tg_ref[pl.ds(step_ref[s], 1), :] += slot_ref[pl.ds(s, 1), :]
        return 0

    lax.fori_loop(0, slots, finish, 0)

    vg_ref[...] = vgin_ref[...]
    for v, a in ((0, 0), (1, 1), (8, 2)):
        vg_ref[v : v + 1, :] = jnp.sum(acc_ref[a], axis=0, keepdims=True)
    lane = lax.broadcasted_iota(jnp.int32, (8, WIDTH), 1)
    zero = jnp.zeros((8, WIDTH), F32)
    short = vg_ref[0:8, :]
    gone = jnp.broadcast_to(vg_ref[8:9, :], (8, WIDTH))
    first_row = lax.broadcasted_iota(jnp.int32, (8, WIDTH), 0) == 0
    for q in range(32):
        d = device_of(jnp.int32(q), me)
        dst = keep_ref if q < 16 else send_ref
        back = (WIDTH - d * 16) & (WIDTH - 1)
        a = jnp.where(lane < 16, pltpu.roll(short, back, 1), zero)
        b = jnp.where((lane < 16) & first_row, pltpu.roll(gone, back, 1), zero)
        wide = jnp.broadcast_to(vg_ref[pl.ds(9 + (d >> 3), 1), :], (8, WIDTH))
        wide = pltpu.roll(wide, (WIDTH - (d & 7) * 64) & (WIDTH - 1), 1)
        w = jnp.where((lane < 64) & first_row, wide, zero)
        a = a + jnp.concatenate([zero[:, 0:128], b[:, 0:128], w[:, 0:128], zero[:, 0:128]], axis=1)
        t = tg_ref[rows_at(d * 8, 8, 8), :]
        dst[q & 15] = jnp.concatenate([t, a], axis=0).astype(BF16)
    for s in range(slots):
        for j in range(4):
            pl.when(j < cnt_ref[s])(lambda s=s, j=j: unit(s, j).wait())


def pair_body(keep, got, *outs):
    for k, o in enumerate(outs):
        part = slice(4 * k, 4 * k + 4)
        o[...] = (keep[part].astype(F32) + got[part].astype(F32)).astype(BF16)


def plane_body(a, b, c, d, *outs):
    for k, o in enumerate(outs):
        o[...] = (
            (a[k].astype(F32) + b[k].astype(F32)) + (c[k].astype(F32) + d[k].astype(F32))
        ).astype(BF16)


def line_sum(a, b, c, d, lo, hi):
    at = slice(lo, hi)
    return (a[at].astype(F32) + b[at].astype(F32)) + (c[at].astype(F32) + d[at].astype(F32))


def end_mlp_body(a, b, c, d, up, down):
    for k in range(4):
        up[:, k * WIDTH : (k + 1) * WIDTH] = line_sum(a, b, c, d, 16 * k, 16 * k + 16)
    down[...] = line_sum(a, b, c, d, 64, 128)


def end_qkv_body(a, b, c, d, qkv, proj):
    for k in range(3):
        qkv[:, k * WIDTH : (k + 1) * WIDTH] = line_sum(a, b, c, d, 16 * k, 16 * k + 16)
    proj[...] = line_sum(a, b, c, d, 48, 64)


def end_small_body(a, b, c, d, time, *vecs):
    tail = line_sum(a, b, c, d, 0, 16)
    time[...] = tail[0:8]
    for v in range(8):
        vecs[v][...] = tail[8 + v, 0:16]
    vecs[8][...] = tail[8, 128:144]
    vecs[9][...] = tail[8, 256:320]


SMEM = pl.BlockSpec(memory_space=pltpu.SMEM)
VMEM = pl.BlockSpec(memory_space=pltpu.VMEM)
ANY = pl.BlockSpec(memory_space=pl.ANY)


def call(body, ins, outs, scratch, args, alias=None, name=None):
    return pl.pallas_call(
        body,
        out_shape=[jax.ShapeDtypeStruct(s, d) for s, d, _ in outs],
        in_specs=list(ins),
        out_specs=[m for _, _, m in outs],
        scratch_shapes=scratch,
        input_output_aliases=alias or {},
        compiler_params=pltpu.CompilerParams(vmem_limit_bytes=VMEM_BYTES),
        name=name,
    )(*args)


def dma(*shape):
    return pltpu.SemaphoreType.DMA(shape)


def vm(*shape, dtype=BF16):
    return pltpu.VMEM(shape, dtype)


def ints(n):
    return pltpu.SMEM((n,), jnp.int32)


def pack_rows(lengths, validity, cotangent, absorbed):
    slots, length, width = cotangent.shape
    return call(
        pack_body,
        [SMEM] * 2 + [VMEM] * 2,
        [
            ((slots * length, width), BF16, VMEM),
            (cotangent.shape, BF16, VMEM),
            ((slots, width), F32, VMEM),
            ((8, width), F32, VMEM),
        ],
        [ints(slots), ints(slots)],
        (lengths, validity, cotangent, absorbed),
        name="pack_rows",
    )


def front(me, lengths, validity, timesteps, inputs, absorbed, blocks, t_rows):
    slots, length, width = inputs.shape
    rows = slots * length
    return call(
        front_body,
        [SMEM] * 4 + [VMEM, ANY] + [VMEM] * 8,
        [
            ((rows, width), F32, ANY),
            ((rows, width), BF16, ANY),
            ((rows, 3 * width), BF16, ANY),
            ((rows, width), BF16, ANY),
            ((slots, HEADS, length), F32, VMEM),
            ((slots, length, width), BF16, ANY),
            ((16, width), F32, VMEM),
        ],
        [
            vm(slots, length, width),
            vm(rows, width, dtype=F32),
            vm(rows, width),
            vm(rows, 3 * width),
            vm(rows, width),
            vm(slots, length, width),
            vm(width, 3 * width),
            vm(t_rows, width, dtype=F32),
            vm(width, length),
            vm(HEADS, 80, length),
            vm(HEADS, length, length, dtype=F32),
            vm(HEADS, length, length),
            ints(slots),
            ints(slots),
            dma(slots),
            dma(8),
            dma(8),
            dma(8),
            dma(8),
            dma(slots),
        ],
        (me, lengths, validity, timesteps, absorbed, inputs, *blocks),
        name="front",
    )


def up_part(me, lengths, validity, mix, start, cp, vec, blocks):
    rows, width = cp.shape
    slots = lengths.shape[0]
    return call(
        up_body,
        [SMEM] * 3 + [VMEM] + [ANY] * 3 + [VMEM] * 8,
        [
            ((rows, width), F32, ANY),
            ((rows, FF), BF16, ANY),
            ((rows, FF), BF16, ANY),
            ((16, 128, width), BF16, VMEM),
            ((16, 128, width), BF16, VMEM),
            ((16, width), F32, VMEM),
        ],
        [
            vm(rows, width),
            vm(rows, width, dtype=F32),
            vm(rows, width),
            vm(rows, width),
            vm(rows, FF),
            vm(rows, FF),
            vm(2, TILE, FFC, dtype=F32),
            vm(2, TILE, FFC, dtype=F32),
            vm(width, FF),
            vm(FF, width),
            vm(width, width),
            vm(width, FFC, dtype=F32),
            vm(FFC, width, dtype=F32),
            vm(8, FF, dtype=F32),
            vm(8, width, dtype=F32),
            ints(slots),
            ints(slots),
        ]
        + [dma(8)] * 6,
        (me, lengths, validity, vec, mix, start, cp, *blocks),
        name="up_part",
    )


def down_part(me, lengths, validity, mix, mid, cp, act, gh, vec, vg, out0, blocks):
    slots, length, width = out0.shape
    rows = slots * length
    return call(
        down_body,
        [SMEM] * 3 + [VMEM] * 2 + [ANY] * 6 + [VMEM] * 8,
        [
            ((slots, length, width), BF16, ANY),
            ((rows, width), F32, ANY),
            ((rows, width), BF16, ANY),
            ((width, width), BF16, VMEM),
            ((16, width), F32, VMEM),
        ],
        [
            vm(rows, width),
            vm(rows, width, dtype=F32),
            vm(rows, width),
            vm(rows, FF),
            vm(rows, FF),
            vm(rows, width),
            vm(rows, width),
            vm(rows, width),
            vm(width, FF),
            vm(FF, width),
            vm(width, width),
            vm(3, 8, width, dtype=F32),
            ints(slots),
            ints(slots),
        ]
        + [dma(8)] * 7
        + [dma(slots, 4)],
        (me, lengths, validity, vec, vg, mix, mid, cp, act, gh, out0, *blocks),
        alias={10: 0},
        name="down_part",
    )


def attn_back(lengths, validity, lse, qkv, gmix):
    rows, wide = qkv.shape
    slots, _, length = lse.shape
    width = gmix.shape[1]
    return call(
        attn_body,
        [SMEM] * 2 + [VMEM] + [ANY] * 2,
        [((rows, wide), BF16, ANY)],
        [
            vm(rows, wide),
            vm(rows, width),
            vm(rows, wide),
            vm(width, length),
            vm(HEADS, length, length, dtype=F32),
            vm(HEADS, length, length, dtype=F32),
            vm(HEADS, length, length),
            vm(HEADS, length, length),
            ints(slots),
            ints(slots),
            dma(8),
            dma(8),
            dma(slots),
        ],
        (lengths, validity, lse, qkv, gmix),
        name="attn_back",
    )[0]


def qkv_weights(me, lengths, validity, gpi, n1, dwp, vg):
    rows, width = n1.shape
    slots = lengths.shape[0]
    return call(
        weights_body,
        [SMEM] * 3 + [VMEM] * 2 + [ANY] * 2,
        [
            ((16, 64, width), BF16, VMEM),
            ((16, 64, width), BF16, VMEM),
            ((16, width), F32, VMEM),
        ],
        [
            vm(rows, 3 * width),
            vm(rows, width),
            vm(width, width, dtype=F32),
            vm(3, 8, width, dtype=F32),
            ints(slots),
            ints(slots),
            dma(8),
            dma(8),
        ],
        (me, lengths, validity, dwp, vg, gpi, n1),
        name="qkv_weights",
    )


def back(
    me, lengths, validity, timesteps, gpi, start, gmid, cot, ig0, absorbed, vec, vg, ssum, asum,
    blocks, t_rows,
):
    slots, length, width = cot.shape
    rows = slots * length
    return call(
        back_body,
        [SMEM] * 4 + [VMEM] * 5 + [ANY] * 5 + [VMEM] * 8,
        [
            ((slots, length, width), BF16, ANY),
            ((16, 16, width), BF16, VMEM),
            ((16, 16, width), BF16, VMEM),
        ],
        [
            vm(rows, 3 * width),
            vm(rows, width, dtype=F32),
            vm(rows, width, dtype=F32),
            vm(slots, UNIT, width),
            vm(rows, width),
            vm(width, 3 * width),
            vm(16, width, dtype=F32),
            vm(t_rows, width, dtype=F32),
            vm(slots, width, dtype=F32),
            vm(3, 8, width, dtype=F32),
            ints(slots),
            ints(slots),
            dma(8),
            dma(8),
            dma(8),
            pltpu.SemaphoreType.DMA,
            dma(slots, 4),
        ],
        (
            me, lengths, validity, timesteps, absorbed, vec, vg, ssum, asum,
            gpi, start, gmid, cot, ig0, *blocks,
        ),
        alias={13: 0},
        name="back",
    )


def hop(x, mask):
    return lax.ppermute(x, AXES, [(i, i ^ mask) for i in range(32)])


def join(parts, name):
    return call(
        join_body,
        [VMEM] * 4,
        [((4,) + parts[0].shape, BF16, VMEM)],
        [],
        parts,
        name=name,
    )[0]


def line(x):
    return [hop(x, m) for m in (2, 4, 6)]


def plane(b):
    return [hop(b, m) for m in (8, 16, 24)]


def pair(parts):
    return [hop(p, 1) for p in parts]


def fence(*groups):
    flat = lax.optimization_barrier(tuple(x for g in groups for x in g))
    out, at = [], 0
    for g in groups:
        out.append(list(flat[at : at + len(g)]))
        at += len(g)
    return out


def add_pair(keep, got, name):
    shape = (4,) + keep.shape[1:]
    return call(pair_body, [VMEM] * 2, [(shape, BF16, VMEM)] * 4, [], (keep, got), name=name)


def add_plane(own, got, name):
    shape = own.shape[1:]
    return call(plane_body, [VMEM] * 4, [(shape, BF16, VMEM)] * 4, [], [own] + got, name=name)


def to_plane(parts):
    return [hop(parts[k], 8 * k) for k in (1, 2, 3)]


def to_line(parts):
    return [hop(parts[k], 2 * k) for k in (1, 2, 3)]


def shards(
    n_dev,
    inputs,
    lengths,
    validity,
    absorbed,
    timesteps,
    attn_gain,
    attn_shift,
    query_key_value_weight,
    query_bias,
    value_bias,
    output_projection_weight,
    output_projection_bias,
    mlp_gain,
    mlp_shift,
    up_projection_weight,
    hidden_units_bias,
    down_projection_weight,
    down_output_bias,
    absorb_vector,
    time_table,
    cotangent,
):
    t_rows = time_table.shape[0] * n_dev
    vectors = [
        attn_gain, attn_shift, query_bias, value_bias, output_projection_bias,
        mlp_gain, mlp_shift, down_output_bias, absorb_vector, hidden_units_bias,
    ]
    weights = [
        query_key_value_weight, time_table, up_projection_weight, down_projection_weight,
        output_projection_weight,
    ]

    if n_dev == 32:
        me = lax.axis_index(AXES).astype(jnp.int32)
        one, two = call(
            block_body,
            [VMEM] * 15,
            [((ROWS1, WIDTH), BF16, VMEM), ((ROWS2, WIDTH), BF16, VMEM)],
            [vm(16, WIDTH, dtype=F32)],
            weights + [v.reshape(1, -1) for v in vectors],
            name="blocks",
        )
        got = line(one)
        packed = pack_rows(lengths, validity, cotangent, absorbed)
        got, packed = fence(got, packed)
        cp, ig0, ssum, asum = packed
        own1 = join([one] + got, "join1")
        (own1, two), = fence([own1, two])
        plane1, line2 = fence(plane(own1), line(two))
        plane1 = [own1] + plane1
        other1 = pair(plane1)
        own2 = join([two] + line2, "join2")
        plane2 = [own2] + plane(own2)
        blocks1 = plane1 + other1
    else:
        me = jnp.int32(0)

        def whole(x):
            full = lax.all_gather(x, AXES, axis=0, tiled=True)
            return full.reshape((32, full.shape[0] // 32) + full.shape[1:])

        qkv_all, time_all, up_all, down_all, proj_all = [whole(w) for w in weights]
        vec_all = [whole(v) for v in vectors]
        tail = jnp.zeros((32, 8, WIDTH), BF16)
        for v in range(8):
            tail = tail.at[:, v, 0:16].set(vec_all[v])
        tail = tail.at[:, 0, 128:144].set(vec_all[8])
        tail = tail.at[:, 0, 256:320].set(vec_all[9])
        cut = lambda w: [w[:, :, c : c + WIDTH] for c in range(0, w.shape[2], WIDTH)]
        one = jnp.concatenate(cut(qkv_all) + [time_all, tail], axis=1)
        two = jnp.concatenate(cut(up_all) + [down_all, proj_all], axis=1)
        blocks1 = [one[i::2][4 * k : 4 * k + 4] for i in range(2) for k in range(4)]
        blocks2 = [two[i::2][4 * k : 4 * k + 4] for i in range(2) for k in range(4)]
        cp, ig0, ssum, asum = pack_rows(lengths, validity, cotangent, absorbed)
    me = me.reshape(1)
    start, n1, qkv, mix, lse, out0, vec = front(
        me, lengths, validity, timesteps, inputs, absorbed, blocks1, t_rows
    )
    if n_dev == 32:
        plane2, (start, mix) = fence(plane2, [start, mix])
        blocks2 = plane2 + pair(plane2)
    mid, act, gh, keep2, send2, vg = up_part(me, lengths, validity, mix, start, cp, vec, blocks2)
    if n_dev == 32:
        got2 = hop(send2, 1)
    output, gmid, gmix, dwp, vg = down_part(
        me, lengths, validity, mix, mid, cp, act, gh, vec, vg, out0, blocks2
    )
    if n_dev == 32:
        (got2, gmix), = fence([got2, gmix])
        sum2 = add_pair(keep2, got2, "pair2")
        sum2, (gmix,) = fence(sum2, [gmix])
        got2 = to_plane(sum2)
    gpi = attn_back(lengths, validity, lse, qkv, gmix)
    keep1, send1, vg = qkv_weights(me, lengths, validity, gpi, n1, dwp, vg)
    if n_dev == 32:
        got2, (keep1, send1, gpi) = fence(got2, [keep1, send1, gpi])
        got1 = hop(send1, 1)
        row2 = add_plane(sum2[0], got2, "plane2")
        sum1 = add_pair(keep1, got1, "pair1")
        sum1, row2, (gpi,) = fence(sum1, row2, [gpi])
        got1, got2 = to_plane(sum1), to_line(row2)
    input_grad, keep0, send0 = back(
        me, lengths, validity, timesteps, gpi, start, gmid, cotangent, ig0, absorbed,
        vec, vg, ssum, asum, blocks1, t_rows,
    )
    wide = query_key_value_weight.shape[1]
    ff = up_projection_weight.shape[1]
    if n_dev == 32:
        got1, got2, (keep0, send0) = fence(got1, got2, [keep0, send0])
        got0 = hop(send0, 1)
        row1 = add_plane(sum1[0], got1, "plane1")
        (got0,), row1 = fence([got0], row1)
        sum0 = add_pair(keep0, got0, "pair0")
        got1 = to_line(row1)
        got0 = to_plane(sum0)
        g_up, g_down = call(
            end_mlp_body,
            [VMEM] * 4,
            [((16, ff), F32, VMEM), ((64, WIDTH), F32, VMEM)],
            [],
            [row2[0]] + got2,
            name="end2",
        )
        row0 = add_plane(sum0[0], got0, "plane0")
        got0 = to_line(row0)
        g_qkv, g_proj = call(
            end_qkv_body,
            [VMEM] * 4,
            [((16, wide), F32, VMEM), ((16, WIDTH), F32, VMEM)],
            [],
            [row1[0]] + got1,
            name="end1",
        )
        g_time, *small = call(
            end_small_body,
            [VMEM] * 4,
            [((8, WIDTH), F32, VMEM)] + [((16,), F32, VMEM)] * 9 + [((64,), F32, VMEM)],
            [],
            [row0[0]] + got0,
            name="end0",
        )
    else:
        g0, g1, g2 = [
            jnp.stack([a, b], 1).reshape((32,) + a.shape[1:]).astype(F32)
            for a, b in ((keep0, send0), (keep1, send1), (keep2, send2))
        ]

        def columns(g, n):
            g = jnp.concatenate([g[:, 16 * c : 16 * c + 16] for c in range(n)], axis=2)
            return g.reshape(-1, n * WIDTH)

        g_qkv, g_up = columns(g1, wide // WIDTH), columns(g2, ff // WIDTH)
        g_down, g_proj = g2[:, 64:128].reshape(-1, WIDTH), g1[:, 48:64].reshape(-1, WIDTH)
        g_time = g0[:, 0:8].reshape(-1, WIDTH)
        small = [g0[:, 8 + v, 0:16].reshape(-1) for v in range(8)]
        small += [g0[:, 8, 128:144].reshape(-1), g0[:, 8, 256:320].reshape(-1)]
    grads = [
        small[0], small[1], g_qkv, small[2], small[3], g_proj, small[4], small[5], small[6],
        g_up, small[9], g_down, small[7], small[8], g_time,
    ]
    if n_dev != 32:
        grads = [lax.psum_scatter(g, AXES, scatter_dimension=0, tiled=True) for g in grads]
    return (output, input_grad) + tuple(grads)


def solution(mesh):
    lead = P(AXES)
    n_dev = mesh.shape["dp"] * mesh.shape["fsdp"]
    return jax.shard_map(
        functools.partial(shards, n_dev),
        mesh=mesh,
        in_specs=(lead,) * 21,
        out_specs=(lead,) * 17,
        check_vma=False,
    )
```
